256 devices in a mesh: head: 16 (over z, core), seq: 16 (over y, x).
Axes of the slice: x: 4, y: 4, z: 8, core: 2. Of those that a mesh axis runs over, the one named last changes fastest.
Arguments:
- projected: bfloat16 [32768, 3, 2048], P(('seq', 'head'))
- query_gain: float32 [128], replicated, may hold values from 1.2 to 2
- key_gain: float32 [128], replicated, may hold values from 1.2 to 2
- tile_lists: int32 [16, 256, 96], P('head'), may hold values from 0 to 255, as said below
- tile_counts: int32 [16, 256], P('head'), may hold values from 1 to 96, as said below
Outputs:
- attended: bfloat16 [32768, 2048], P(('seq', 'head'))
The draws below stay inside these ranges and needn't reach their ends.
Inputs may be any that keep to these rules, and one draw needn't show every extreme that they name: `tile_lists`: for each head and query tile the first tile_counts entries are distinct key tile numbers; later entries are tile numbers that carry no meaning. Tile k lies in frame k * 128 // 2048; a live entry whose frame is more than 4 frames from the query tile's frame is among the first 4 tiles of its frame. tile_counts[h, t] is the number of live entries of tile_lists[h, t]; some query tile of some head has 96 in every draw.
All inputs are finite; a program needn't handle non-finite values.
Results may differ from the reference program's by a relative error of at most 0.012.
The reference program's roundings to bfloat16 on the way count: a program that leaves them out, or rounds other values in their place, can miss the bound.
Values may be sent and summed in bfloat16 or wider, within the bound.
A program may use at most 128 MiB of HBM per device.

```python
import math
import jax
import jax.numpy as jnp
from jax import lax

HD = 128
HEADS = 16
TOKENS = 32768
TILE = 128
FRAME_TOK = 2048
GW = 64
NT = 256
MAXK = 96
NEAR = 4
FAR = 4


def radial_lists(key):
    frames = TOKENS // FRAME_TOK
    per_frame = FRAME_TOK // TILE
    tile_total = TOKENS // TILE
    step_total = 2 * frames - 1
    k_rate, k_head, k_jit, k_cap = jax.random.split(key, 4)
    rates = jax.random.randint(k_rate, (HEADS,), 1, max(2, frames // 2) + 1)
    slow_head = jax.random.randint(k_head, (), 0, HEADS)
    rates = jnp.where(jnp.arange(HEADS) == slow_head, frames, rates)
    order_index = jnp.arange(step_total, dtype=jnp.int32)
    distance = (order_index + 1) // 2
    signed = jnp.where(order_index % 2 == 1, distance, -distance)
    tile_ids = jnp.arange(tile_total, dtype=jnp.int32)
    frame_q = tile_ids // per_frame
    spot_q = tile_ids % per_frame
    frame_k = frame_q[:, None] + signed[None, :]
    frame_ok = (frame_k >= 0) & (frame_k < frames)
    far_step = distance > NEAR
    shifts = jnp.minimum(distance[None, :] // rates[:, None], 20)
    starting_width = jnp.maximum(jnp.right_shift(jnp.int32(per_frame), shifts), 1)
    tile_span_width = jnp.where(far_step[None, :], jnp.minimum(starting_width, FAR), starting_width)
    jitter = jax.random.randint(k_jit, (HEADS, tile_total, step_total), 0, per_frame)
    offsets = jnp.arange(per_frame, dtype=jnp.int32)
    spot_near = (spot_q[None, :, None, None] + jitter[..., None] + offsets[None, None, None, :]) % per_frame
    spot_far = (jitter[..., None] + offsets[None, None, None, :]) % FAR
    far_flag = jnp.broadcast_to(far_step[None, None, :, None], spot_near.shape)
    spot_k = jnp.where(far_flag, spot_far, spot_near)
    all_ids = jnp.clip(frame_k, 0, frames - 1)[None, :, :, None] * per_frame + spot_k
    usable = frame_ok[None, :, :, None] & (offsets[None, None, None, :] < tile_span_width[:, None, :, None])
    all_ids = all_ids.reshape(HEADS, tile_total, step_total * per_frame)
    far_flag = far_flag.reshape(HEADS, tile_total, step_total * per_frame)
    usable = usable.reshape(HEADS, tile_total, step_total * per_frame)
    priority = jnp.where(usable & far_flag, 0, jnp.where(usable, 1, 2))
    rank_key = priority * (step_total * per_frame) + jnp.arange(step_total * per_frame, dtype=jnp.int32)
    picked = jnp.argsort(rank_key, axis=-1)[..., :MAXK]
    chosen_lists = jnp.take_along_axis(all_ids, picked, axis=-1).astype(jnp.int32)
    caps = jax.random.randint(k_cap, (HEADS, tile_total), MAXK // 2, MAXK + 1)
    forced = (jnp.arange(HEADS, dtype=jnp.int32)[:, None] == slow_head) & (tile_ids[None, :] == 0)
    caps = jnp.where(forced, MAXK, caps)
    chosen_counts = jnp.minimum(jnp.sum(usable.astype(jnp.int32), -1), caps).astype(jnp.int32)
    return (chosen_lists, chosen_counts)


def draw_tile_lists(key, part):
    return radial_lists(key)[0]


def draw_tile_counts(key, part):
    return radial_lists(key)[1]


def draw_projected(key, part):
    key = jax.random.fold_in(key, 7)
    key_base, key_rows, key_cols = jax.random.split(key, 3)
    full_shape = (TOKENS, 3, HEADS * HD)
    base_values = jax.random.normal(key_base, full_shape, jnp.float32)
    spread = 1.15
    row_scale = jnp.exp(jax.random.uniform(key_rows, (TOKENS, 3, 1), jnp.float32, -spread, spread))
    col_scale = jnp.exp(jax.random.uniform(key_cols, (1, 3, HEADS * HD), jnp.float32, -spread, spread))
    return (base_values * row_scale * col_scale).astype(jnp.bfloat16)


def setup_inputs(seed: int = 0) -> dict:
    seeds = jax.random.split(jax.random.key(seed), 6)
    return {
        "projected": draw_projected(jax.random.fold_in(seeds[5], 71), 0),
        "query_gain": jnp.clip(jax.random.uniform(seeds[1], (HD,), jnp.float32, 1.2, 2.0), 1.2, 2.0),
        "key_gain": jnp.clip(jax.random.uniform(seeds[2], (HD,), jnp.float32, 1.2, 2.0), 1.2, 2.0),
        "tile_lists": draw_tile_lists(jax.random.fold_in(seeds[5], 71), 0),
        "tile_counts": draw_tile_counts(jax.random.fold_in(seeds[5], 71), 0),
    }


ROPE_THETA = 256.0

def norm_rope(field, gain, positions):
    field = field * lax.rsqrt(lax.optimization_barrier(jnp.mean(field * field, -1, keepdims=True)) + 1e-06) * gain
    head_size = field.shape[-1]
    frame_index = positions // FRAME_TOK
    remainder = positions % FRAME_TOK
    row_index = remainder // GW
    column = remainder % GW
    width_one = head_size // 8
    width_two = (head_size - width_one) // 2
    extents = (width_one, width_two, head_size - width_one - width_two)
    pieces = []
    offset = 0
    for coordinate, extent in zip((frame_index, row_index, column), extents):
        middle = extent // 2
        inverse = ROPE_THETA ** (-2.0 * jnp.arange(middle, dtype=jnp.float32) / extent)
        angles = coordinate.astype(jnp.float32)[:, None] * inverse[None, :]
        angles = angles.reshape((coordinate.shape[0],) + (1,) * (field.ndim - 2) + (middle,))
        leading = field[..., offset:offset + middle]
        trailing = field[..., offset + middle:offset + extent]
        cosine = jnp.cos(angles)
        sines = jnp.sin(angles)
        pieces.append(leading * cosine - trailing * sines)
        pieces.append(trailing * cosine + leading * sines)
        offset = offset + extent
    return jnp.concatenate(pieces, -1)

def head_attention(operands):
    query_head, key_head, value_head, lists_head, counts_head = operands
    factor = 1.0 / math.sqrt(HD)

    def one_block(block_index):
        start_tile = (block_index * 16).astype(jnp.int32)
        query_block = lax.dynamic_slice_in_dim(query_head, start_tile, 16, 0)
        list_block = lax.dynamic_slice_in_dim(lists_head, start_tile, 16, 0)
        count_block = lax.dynamic_slice_in_dim(counts_head, start_tile, 16, 0)
        key_block = key_head[list_block].reshape(16, MAXK * TILE, HD)
        value_block = value_head[list_block].reshape(16, MAXK * TILE, HD)
        scores = jnp.einsum('tqd,tkd->tqk', query_block.astype(jnp.float32), key_block.astype(jnp.float32), precision=lax.Precision.HIGHEST) * factor
        live_slots = jnp.arange(MAXK, dtype=jnp.int32)[None, :] < count_block[:, None]
        key_valid = jnp.repeat(live_slots, TILE, axis=1)
        weights = jnp.where(key_valid[:, None, :], jnp.exp(scores), 0.0)
        denominator = lax.optimization_barrier(jnp.sum(weights, 2))
        rounded = lax.optimization_barrier(weights.astype(jnp.bfloat16)).astype(jnp.float32)
        numerator = jnp.einsum('tqk,tkd->tqd', rounded, value_block.astype(jnp.float32), precision=lax.Precision.HIGHEST)
        return (numerator / denominator[..., None]).astype(jnp.bfloat16)
    blocks = lax.map(one_block, jnp.arange(NT // 16, dtype=jnp.int32))
    return blocks.reshape(NT, TILE, HD)

def reference(projected, query_gain, key_gain, tile_lists, tile_counts):
    field = projected.astype(jnp.float32).reshape(TOKENS, 3, HEADS, HD)
    positions = jnp.arange(TOKENS, dtype=jnp.int32)
    queries = norm_rope(field[:, 0], query_gain, positions).astype(jnp.bfloat16)
    key_rows = norm_rope(field[:, 1], key_gain, positions).astype(jnp.bfloat16)
    value_rows = projected.reshape(TOKENS, 3, HEADS, HD)[:, 2]

    def by_head(array):
        return jnp.transpose(array, (1, 0, 2)).reshape(HEADS, NT, TILE, HD)
    output_rows = lax.map(head_attention, (by_head(queries), by_head(key_rows), by_head(value_rows), tile_lists, tile_counts))
    output_rows = jnp.transpose(output_rows.reshape(HEADS, TOKENS, HD), (1, 0, 2))
    return output_rows.reshape(TOKENS, HEADS * HD)
```

```python
import functools
import math

import jax
import jax.numpy as jnp
from jax import lax
from jax.experimental import pallas as pl
from jax.experimental.pallas import tpu as pltpu
from jax.sharding import PartitionSpec as P


TILE = 128
HD = 128
GW = 64
HEADS = 16
FRAMES = 16
PER = 16
CH = 4
PAIRS = 8
THETA = 256.0
SCALE = math.log2(math.e) / math.sqrt(HD)
G = 8
SUB = 2
MESH = pl.DeviceIdType.MESH
f32 = jnp.float32
bf16 = jnp.bfloat16


def rope_tables(sq, hd):
    tokens = hd * TILE + jnp.arange(TILE, dtype=jnp.int32)
    row = tokens // GW
    column = tokens % GW
    frame = jnp.full((TILE,), sq, jnp.int32)
    first = HD // 8
    second = (HD - first) // 2
    cosines, sines = [], []
    for coordinate, extent in zip((frame, row, column), (first, second, HD - first - second)):
        middle = extent // 2
        inverse = THETA ** (-2.0 * jnp.arange(middle, dtype=f32) / extent)
        angles = coordinate.astype(f32)[:, None] * inverse[None, :]
        c, s = jnp.cos(angles), jnp.sin(angles)
        cosines += [c, c]
        sines += [-s, s]
    return jnp.concatenate(cosines, 1), jnp.concatenate(sines, 1)


def partner(field):
    lane = lax.broadcasted_iota(jnp.int32, field.shape, 1)
    first = HD // 8
    half = (HD - first) // 4
    near = jnp.where(lane < first // 2, pltpu.roll(field, HD - first // 2, 1), pltpu.roll(field, first // 2, 1))
    offset = lane - first
    lower = (offset < half) | ((offset >= 2 * half) & (offset < 3 * half))
    far = jnp.where(lower, pltpu.roll(field, HD - half, 1), pltpu.roll(field, half, 1))
    return jnp.where(lane < first, near, far)


def prepare_kernel(proj, cos, sin, qg, kg, q_out, kv_out):
    cosine = cos[...]
    sine = sin[...]
    for h in range(HEADS):
        for part, gain in ((0, qg), (1, kg)):
            lo = (part * HEADS + h) * HD
            field = proj[:, lo:lo + HD].astype(f32)
            mean = jnp.sum(field * field, axis=1, keepdims=True) * (1.0 / HD)
            field = field * lax.rsqrt(mean + 1e-06) * gain[...]
            turned = (field * cosine + partner(field) * sine).astype(bf16)
            if part == 0:
                q_out[h] = turned
            else:
                kv_out[h, 0] = turned
        lo = (2 * HEADS + h) * HD
        kv_out[h, 1] = proj[:, lo:lo + HD]


def place():
    hd = lax.axis_index("head")
    sq = lax.axis_index("seq")
    z, c = hd // 2, hd % 2
    y, x = sq // 4, sq % 4
    b, k = x // 2, x % 2
    return hd, sq, z, c, y, x, b, k


def spread_kernel(q_in, kv_in, lists_in, counts_in, q, kv, lists, counts,
                  s1kv, s1q, r1kv, r1q, s2, r2, s3, r3, sl, rl):
    hd, sq, z, c, y, x, b, k = place()
    p = 2 * y + k
    frame = 2 * p + c

    def dev(h, s):
        return {"head": h, "seq": s}

    def pair_dev(pt):
        return dev(hd, 4 * (pt // 2) + 2 * b + pt % 2)

    sibling = dev(2 * z + 1 - c, sq)

    def home(r, bb):
        zt = (z + r) % 8
        return zt, 2 * zt + x % 2, 4 * y + 2 * bb + x // 2

    barrier = pltpu.get_barrier_semaphore()
    for t in range(HEADS):
        @pl.when((t != hd) | (frame != sq))
        def _():
            pl.semaphore_signal(barrier, 1, device_id=dev(t, frame), device_id_type=MESH)
    for d in range(1, PAIRS):
        pl.semaphore_signal(barrier, 1, device_id=pair_dev((p + d) % PAIRS), device_id_type=MESH)
    pl.semaphore_signal(barrier, 1, device_id=sibling, device_id_type=MESH)
    self_home = (frame == sq).astype(jnp.int32)
    pl.semaphore_wait(barrier, HEADS - self_home + PAIRS)

    def phase1(src, dst, send, recv, r, bb, act):
        zt, ht, st = home(r, bb)
        head = 2 * zt + bb
        remote = (ht != hd) | (st != sq)

        @pl.when(remote)
        def _():
            cp = pltpu.make_async_remote_copy(src.at[head], dst, send.at[r * 2 + bb], recv.at[hd],
                                              device_id=dev(ht, st), device_id_type=MESH)
            cp.start() if act else cp.wait_send()

        if act:
            @pl.when(jnp.logical_not(remote))
            def _():
                pltpu.make_async_copy(src.at[head], dst, recv.at[hd]).start()

    kv_home = kv.at[sq * PER + hd]
    q_home = q.at[hd]
    for r in range(8):
        for bb in range(2):
            phase1(kv_in, kv_home, s1kv, r1kv, r, bb, True)
    for r in range(8):
        for bb in range(2):
            phase1(q_in, q_home, s1q, r1q, r, bb, True)

    def list_copies(rows, device):
        return (pltpu.make_async_remote_copy(lists_in.at[pl.ds(rows * PER, PER)], lists, sl.at[0], rl.at[0],
                                             device_id=device, device_id_type=MESH),
                pltpu.make_async_remote_copy(counts_in, counts, sl.at[1], rl.at[1],
                                             device_id=device, device_id_type=MESH))

    @pl.when(b == c)
    def _():
        for cp in list_copies(4 * y + 2 * k + 1 - c, sibling):
            cp.start()
        pltpu.make_async_copy(lists_in.at[pl.ds(frame * PER, PER)], lists, rl.at[0]).start()
        pltpu.make_async_copy(counts_in, counts, rl.at[1]).start()

    def span(fr, m):
        return kv.at[pl.ds(fr * PER + m * CH, CH)]

    def lane_copy(d, m):
        part = span(frame, m)
        return pltpu.make_async_remote_copy(part, part, s2.at[d + PAIRS - 1, m], r2.at[p, m],
                                            device_id=pair_dev(p + d), device_id_type=MESH)

    def lane_arrival(pt, m):
        part = span(2 * pt + c, m)
        return pltpu.make_async_remote_copy(part, part, s2.at[0, 0], r2.at[pt, m],
                                            device_id=sibling, device_id_type=MESH)

    def cross_copy(pt, m, core):
        part = span(2 * pt + core, m)
        return pltpu.make_async_remote_copy(part, part, s3.at[pt, m], r3.at[pt, m],
                                            device_id=sibling, device_id_type=MESH)

    def inside(pt):
        return (pt >= 0) & (pt < PAIRS)

    def crosses(dp, m, core):
        if abs(dp) <= 1:
            return True
        if dp == 2:
            return (core == 0) | (m == 0)
        if dp == -2:
            return (core == 1) | (m == 0)
        return m == 0

    def own(m):
        for t in range(CH):
            j = m * CH + t
            pltpu.make_async_copy(kv.at[frame * PER + j], kv.at[frame * PER + j], r1kv.at[j]).wait()
        for d in (1, -1, 2, -2):
            @pl.when(inside(p + d))
            def _():
                lane_copy(d, m).start()
        cross_copy(p, m, c).start()
        for d in range(3, PAIRS):
            for sgn in (1, -1):
                @pl.when(inside(p + sgn * d) & (m == 0))
                def _():
                    lane_copy(sgn * d, m).start()

    def relay(m):
        for d in (1, -1, 2, -2):
            pt = p + d

            @pl.when(inside(pt))
            def _():
                lane_arrival(pt, m).wait_recv()

            @pl.when(inside(pt) & crosses(d, m, c))
            def _():
                cross_copy(pt, m, c).start()
        for d in range(3, PAIRS):
            for sgn in (1, -1):
                pt = p + sgn * d

                @pl.when(inside(pt) & (m == 0))
                def _():
                    lane_arrival(pt, m).wait_recv()
                    cross_copy(pt, m, c).start()

    order = [(z // 2 + 4 - i) % 4 for i in range(4)]
    own(order[0])
    own(order[1])
    relay(order[0])
    own(order[2])
    relay(order[1])
    own(order[3])
    relay(order[2])
    relay(order[3])

    for j in range(PER):
        pltpu.make_async_copy(q.at[j], q.at[j], r1q.at[j]).wait()
    pltpu.make_async_copy(lists_in.at[pl.ds(frame * PER, PER)], lists, rl.at[0]).wait()
    pltpu.make_async_copy(counts_in, counts, rl.at[1]).wait()

    @pl.when(b == c)
    def _():
        for cp in list_copies(4 * y + 2 * k + 1 - c, sibling):
            cp.wait_send()

    for m in range(4):
        for d in range(1 - PAIRS, PAIRS):
            if d != 0 and (abs(d) <= 2 or m == 0):
                @pl.when(inside(p + d))
                def _():
                    lane_copy(d, m).wait_send()
            if abs(d) <= 2 or m == 0:
                @pl.when(inside(p + d) & crosses(d, m, c))
                def _():
                    cross_copy(p + d, m, c).wait_send()

                @pl.when(inside(p + d) & crosses(d, m, 1 - c))
                def _():
                    cross_copy(p + d, m, 1 - c).wait_recv()
    for r in range(8):
        for bb in range(2):
            phase1(kv_in, kv_home, s1kv, r1kv, r, bb, False)
            phase1(q_in, q_home, s1q, r1q, r, bb, False)


def attend_kernel(lists, counts, q_ref, kv_hbm, o_ref, kv, s0, s1, acc, den, sems):
    _, _, _, c, y, _, _, k = place()
    frame = 4 * y + 2 * k + c

    def loads(act):
        for fr in range(FRAMES):
            near = jnp.abs(fr - frame) <= 4

            @pl.when(near)
            def _():
                part = pl.ds(fr * PER, PER)
                act(pltpu.make_async_copy(kv_hbm.at[part], kv.at[part], sems.at[fr]))

            @pl.when(jnp.logical_not(near))
            def _():
                part = pl.ds(fr * PER, CH)
                act(pltpu.make_async_copy(kv_hbm.at[part], kv.at[part], sems.at[fr]))

    loads(lambda cp: cp.start())
    acc[...] = jnp.zeros_like(acc)
    den[...] = jnp.zeros_like(den)

    def count(i):
        return counts[0, frame * PER + i]

    total = lax.fori_loop(0, PER, lambda i, t: t + (count(i) + G - 1) // G, 0)
    loads(lambda cp: cp.wait())

    def following(i, g):
        stay = ((g + 1) * G < count(i)) | (i == PER - 1)
        return jnp.where(stay, i, i + 1), jnp.where(stay, g + 1, 0)

    def ids(i, g):
        last = count(i) - 1
        return [lists[i, jnp.minimum(g * G + u, last)] for u in range(G)]

    def score(i, g, s):
        chosen = ids(i, g)
        q = q_ref[i]
        for w in range(0, G, SUB):
            keys = jnp.concatenate([kv[t, 0] for t in chosen[w:w + SUB]], 0)
            s[:, w * TILE:(w + SUB) * TILE] = lax.dot_general(
                q, keys, (((1,), (1,)), ((), ())), preferred_element_type=f32)

    def weigh(i, g, s):
        chosen = ids(i, g)
        n = count(i)
        d = jnp.zeros((TILE, TILE), f32)
        a = jnp.zeros((TILE, HD), f32)
        for w in range(0, G, SUB):
            e = jnp.exp2(s[:, w * TILE:(w + SUB) * TILE] * SCALE)
            parts = [jnp.where(g * G + w + u < n, e[:, u * TILE:(u + 1) * TILE], 0.0) for u in range(SUB)]
            for part in parts:
                d = d + part
            weights = jnp.concatenate(parts, 1).astype(bf16)
            values = jnp.concatenate([kv[t, 1] for t in chosen[w:w + SUB]], 0)
            a = a + lax.dot_general(weights, values, (((1,), (0,)), ((), ())), preferred_element_type=f32)
        acc[i] += a
        den[i] += d

    zero = jnp.int32(0)
    score(zero, zero, s0)

    def body(_, state):
        i, g = state
        i1, g1 = following(i, g)
        score(i1, g1, s1)
        weigh(i, g, s0)
        i2, g2 = following(i1, g1)
        score(i2, g2, s0)
        weigh(i1, g1, s1)
        return i2, g2

    lax.fori_loop(0, (total + 1) // 2, body, (zero, zero))

    def finish(i, _):
        o_ref[i] = (acc[i] / jnp.sum(den[i], axis=1, keepdims=True)).astype(bf16)
        return 0

    lax.fori_loop(0, PER, finish, 0)


def return_kernel(o_in, out, send, recv):
    hd, sq, z, c, y, x, b, k = place()
    frame = 4 * y + 2 * k + c
    head = 2 * z + b
    barrier = pltpu.get_barrier_semaphore()

    def source(h):
        return 2 * (h // 2) + x % 2, 4 * y + 2 * (h % 2) + x // 2

    self_home = (frame == sq).astype(jnp.int32)
    for h in range(HEADS):
        hs, ss = source(h)

        @pl.when((hs != hd) | (ss != sq))
        def _():
            pl.semaphore_signal(barrier, 1, device_id={"head": hs, "seq": ss}, device_id_type=MESH)
    pl.semaphore_wait(barrier, HEADS - self_home)
    columns = out.at[:, pl.ds(pl.multiple_of(head * HD, HD), HD)]

    def copies(act):
        for r in range(HEADS):
            t = (hd + r) % HEADS
            remote = (t != hd) | (frame != sq)

            @pl.when(remote)
            def _():
                cp = pltpu.make_async_remote_copy(o_in.at[t], columns, send.at[r], recv.at[head],
                                                  device_id={"head": t, "seq": frame}, device_id_type=MESH)
                cp.start() if act else cp.wait_send()

            if act:
                @pl.when(jnp.logical_not(remote))
                def _():
                    pltpu.make_async_copy(o_in.at[t], columns, recv.at[head]).start()

    copies(True)
    for h in range(HEADS):
        part = out.at[:, pl.ds(h * HD, HD)]
        pltpu.make_async_copy(o_in.at[0], part, recv.at[h]).wait()
    copies(False)


def local(projected, query_gain, key_gain, tile_lists, tile_counts):
    hd = lax.axis_index("head")
    sq = lax.axis_index("seq")
    vmem = pl.BlockSpec(memory_space=pltpu.VMEM)
    smem = pl.BlockSpec(memory_space=pltpu.SMEM)
    hbm = pl.BlockSpec(memory_space=pl.ANY)
    sds = jax.ShapeDtypeStruct
    dma = pltpu.SemaphoreType.DMA
    cosine, sine = rope_tables(sq, hd)
    q_own, kv_own = pl.pallas_call(
        prepare_kernel,
        out_shape=(sds((HEADS, TILE, HD), bf16), sds((HEADS, 2, TILE, HD), bf16)),
        in_specs=[vmem] * 5,
        out_specs=(vmem, vmem),
        name="prepare",
    )(projected.reshape(TILE, 3 * HEADS * HD), cosine, sine, query_gain[None], key_gain[None])
    q, kv, lists, counts = pl.pallas_call(
        spread_kernel,
        out_shape=(sds((PER, TILE, HD), bf16), sds((FRAMES * PER, 2, TILE, HD), bf16),
                   sds((PER, 96), jnp.int32), sds((1, FRAMES * PER), jnp.int32)),
        in_specs=[hbm] * 4,
        out_specs=(hbm,) * 4,
        scratch_shapes=[dma((16,)), dma((16,)), dma((16,)), dma((16,)), dma((2 * PAIRS - 1, 4)), dma((PAIRS, 4)),
                        dma((PAIRS, 4)), dma((PAIRS, 4)), dma((2,)), dma((2,))],
        compiler_params=pltpu.CompilerParams(collective_id=0, has_side_effects=True),
        name="spread",
    )(q_own, kv_own, tile_lists[0], tile_counts)
    attended = pl.pallas_call(
        attend_kernel,
        out_shape=sds((PER, TILE, HD), bf16),
        in_specs=[smem, smem, vmem, hbm],
        out_specs=vmem,
        scratch_shapes=[pltpu.VMEM((FRAMES * PER, 2, TILE, HD), bf16), pltpu.VMEM((TILE, G * TILE), f32),
                        pltpu.VMEM((TILE, G * TILE), f32), pltpu.VMEM((PER, TILE, TILE), f32),
                        pltpu.VMEM((PER, TILE, HD), f32), dma((FRAMES,))],
        compiler_params=pltpu.CompilerParams(vmem_limit_bytes=40 * 1024 * 1024),
        name="attend",
    )(lists, counts, q, kv)
    return pl.pallas_call(
        return_kernel,
        out_shape=sds((TILE, HEADS * HD), bf16),
        in_specs=[hbm],
        out_specs=hbm,
        scratch_shapes=[dma((HEADS,)), dma((HEADS,))],
        compiler_params=pltpu.CompilerParams(collective_id=1, has_side_effects=True),
        name="give_back",
    )(attended)


def solution(mesh):
    in_specs = (P(("seq", "head"), None, None), P(), P(), P("head", None, None), P("head", None))
    return jax.shard_map(local, mesh=mesh, in_specs=in_specs, out_specs=P(("seq", "head"), None), check_vma=False)
```

```python
import functools
import math

import jax
import jax.numpy as jnp
from jax import lax
from jax.experimental import pallas as pl
from jax.experimental.pallas import tpu as pltpu
from jax.sharding import PartitionSpec as P


TILE = 128
HD = 128
GW = 64
HEADS = 16
FRAMES = 16
PER = 16
CH = 4
THETA = 256.0
SCALE = math.log2(math.e) / math.sqrt(HD)
G = 8
SUB = 2
HOPS = (0, 1, -1, 2, -2, 3, -3, 4)
MESH = pl.DeviceIdType.MESH
f32 = jnp.float32
bf16 = jnp.bfloat16


def rope_tables(sq, hd):
    tokens = hd * TILE + jnp.arange(TILE, dtype=jnp.int32)
    row = tokens // GW
    column = tokens % GW
    frame = jnp.full((TILE,), sq, jnp.int32)
    first = HD // 8
    second = (HD - first) // 2
    cosines, sines = [], []
    for coordinate, extent in zip((frame, row, column), (first, second, HD - first - second)):
        middle = extent // 2
        inverse = THETA ** (-2.0 * jnp.arange(middle, dtype=f32) / extent)
        angles = coordinate.astype(f32)[:, None] * inverse[None, :]
        c, s = jnp.cos(angles), jnp.sin(angles)
        cosines += [c, c]
        sines += [-s, s]
    return jnp.concatenate(cosines, 1), jnp.concatenate(sines, 1)


def partner(field):
    lane = lax.broadcasted_iota(jnp.int32, field.shape, 1)
    first = HD // 8
    half = (HD - first) // 4
    near = jnp.where(lane < first // 2, pltpu.roll(field, HD - first // 2, 1), pltpu.roll(field, first // 2, 1))
    offset = lane - first
    lower = (offset < half) | ((offset >= 2 * half) & (offset < 3 * half))
    far = jnp.where(lower, pltpu.roll(field, HD - half, 1), pltpu.roll(field, half, 1))
    return jnp.where(lane < first, near, far)


def prepare_kernel(proj, cos, sin, qg, kg, q_out, kv_out):
    cosine = cos[...]
    sine = sin[...]
    for h in range(HEADS):
        for part, gain in ((0, qg), (1, kg)):
            lo = h * HD
            field = proj[part, :, lo:lo + HD].astype(f32)
            mean = jnp.sum(field * field, axis=1, keepdims=True) * (1.0 / HD)
            field = field * lax.rsqrt(mean + 1e-06) * gain[...]
            turned = (field * cosine + partner(field) * sine).astype(bf16)
            if part == 0:
                q_out[h] = turned
            else:
                kv_out[h, 0] = turned
        kv_out[h, 1] = proj[2, :, h * HD:(h + 1) * HD]


def place():
    hd = lax.axis_index("head")
    sq = lax.axis_index("seq")
    z, c = hd // 2, hd % 2
    y, x = sq // 4, sq % 4
    b, k = x // 2, x % 2
    return hd, sq, z, c, y, x, b, k


def spread_kernel(q_in, kv_in, lists_in, counts_in, q, kv, transit, lists, counts,
                  sz, st, sq_sem, rz, rt, rq, s_mate, s_far, s_y, s_relay, s_cross, arrive, sl, rl):
    hd, sq, z, c, y, x, b, k = place()
    frame = 4 * y + 2 * k + c
    started = []

    def dev(h, s):
        return {"head": h, "seq": s}

    def send(pred, make):
        @pl.when(pred)
        def _():
            make().start()
        started.append((pred, make))

    sibling = dev(2 * z + 1 - c, sq)
    mate = dev(hd, 4 * y + 2 * b + 1 - k)
    opposite = dev(hd, 4 * y + 3 - x)
    row_up, row_down, row_two = (y + 1) % 4, (y + 3) % 4, (y + 2) % 4
    up = dev(hd, 4 * row_up + x)
    down = dev(hd, 4 * row_down + x)

    barrier = pltpu.get_barrier_semaphore()
    for t in range(1, HEADS):
        pl.semaphore_signal(barrier, 1, device_id=dev((hd + t) % HEADS, sq), device_id_type=MESH)
    for device in (mate, opposite, up, down):
        pl.semaphore_signal(barrier, 1, device_id=device, device_id_type=MESH)
    for t in range(HEADS):
        @pl.when((t != hd) | (frame != sq))
        def _():
            pl.semaphore_signal(barrier, 1, device_id=dev(t, frame), device_id_type=MESH)
    self_home = (frame == sq).astype(jnp.int32)
    pl.semaphore_wait(barrier, HEADS - 1 + 4 + HEADS - self_home)

    def line(src, dst, send_sem, recv_sem, target, seq):
        remote = (target != hd) | (seq != sq)
        send(remote, lambda: pltpu.make_async_remote_copy(src, dst, send_sem, recv_sem,
                                                          device_id=dev(target, seq), device_id_type=MESH))

        @pl.when(jnp.logical_not(remote))
        def _():
            pltpu.make_async_copy(src, dst, recv_sem).start()

    for r, hop in enumerate(HOPS):
        zt = (z + hop + 8) % 8
        line(kv_in.at[2 * zt + b], kv.at[sq * PER + hd], sz.at[r], rz.at[hd], 2 * zt + k, sq)
        line(kv_in.at[2 * zt + 1 - b], transit.at[hd], st.at[r], rt.at[hd], 2 * zt + k, sq)
    for r, hop in enumerate(HOPS):
        zt = (z + hop + 8) % 8
        for bb in range(2):
            line(q_in.at[2 * zt + bb], q.at[hd], sq_sem.at[2 * r + bb], rq.at[hd], 2 * zt + k, 4 * y + 2 * bb + b)

    mine = b == c
    other_rows = lists_in.at[pl.ds((4 * y + 2 * k + 1 - c) * PER, PER)]
    my_rows = lists_in.at[pl.ds(frame * PER, PER)]
    send(mine, lambda: pltpu.make_async_remote_copy(other_rows, lists, sl.at[0], rl.at[0],
                                                    device_id=sibling, device_id_type=MESH))
    send(mine, lambda: pltpu.make_async_remote_copy(counts_in, counts, sl.at[1], rl.at[1],
                                                    device_id=sibling, device_id_type=MESH))

    @pl.when(mine)
    def _():
        pltpu.make_async_copy(my_rows, lists, rl.at[0]).start()
        pltpu.make_async_copy(counts_in, counts, rl.at[1]).start()

    def span(fr, m):
        return kv.at[pl.ds(fr * PER + m * CH, CH)]

    def chunk(src, fr, m, sem, device):
        return pltpu.make_async_remote_copy(src, span(fr, m), sem, arrive.at[fr, m],
                                            device_id=device, device_id_type=MESH)

    def arrived(pred, fr, m):
        @pl.when(pred)
        def _():
            pltpu.make_async_copy(span(fr, m), span(fr, m), arrive.at[fr, m]).wait()

    def cross(pred, fr, m):
        send(pred, lambda: chunk(span(fr, m), fr, m, s_cross.at[fr, m], sibling))

    def down_received(first, m):
        return (m == 0) | ((y > 0) & (k == 0)) if first else (m == 0) | (y > 0)

    def up_received(first, m):
        return (m == 0) | (y < 3) if first else (m == 0) | ((y < 3) & (k == 1))

    def down_crosses(first, m, core):
        if first:
            return (m == 0) | ((y > 0) & (k == 0) & (core == 1))
        return (m == 0) | ((y > 0) & ((k == 0) | (core == 1)))

    def up_crosses(first, m, core):
        if first:
            return (m == 0) | ((y < 3) & ((k == 1) | (core == 0)))
        return (m == 0) | ((y < 3) & (k == 1) & (core == 0))

    own = 4 * y + 2 * b + c
    guest = 4 * y + 2 * (1 - b) + c
    lands = k == c
    relays = k != c

    def from_here(fr, first, slot, m):
        send((m == 0) | ((y < 3) & ((k == 0) | jnp.logical_not(first))),
             lambda: chunk(span(fr, m), fr, m, s_y.at[slot, 0, m], up))
        send((m == 0) | ((y > 0) & ((k == 1) | first)),
             lambda: chunk(span(fr, m), fr, m, s_y.at[slot, 1, m], down))
        cross(True, fr, m)

    def step_own(m):
        @pl.when(lands)
        def _():
            for t in range(CH):
                j = m * CH + t
                pltpu.make_async_copy(kv.at[own * PER + j], kv.at[own * PER + j], rz.at[j]).wait()
        arrived(relays, own, m)
        send(lands, lambda: chunk(span(own, m), own, m, s_mate.at[m], mate))

        @pl.when(lands)
        def _():
            for t in range(CH):
                j = m * CH + t
                pltpu.make_async_copy(transit.at[j], transit.at[j], rt.at[j]).wait()
        send(lands, lambda: chunk(transit.at[pl.ds(m * CH, CH)], own, m, s_far.at[m], opposite))
        from_here(own, b == 0, 0, m)

    def step_guest(m):
        arrived(True, guest, m)
        send(relays, lambda: chunk(span(guest, m), guest, m, s_mate.at[m], mate))
        from_here(guest, b == 1, 1, m)

    def step_rows(m):
        for first in (True, False):
            fr = 4 * row_down + c + (0 if first else 2)
            arrived(down_received(first, m), fr, m)
            cross(down_crosses(first, m, c), fr, m)
            if first:
                send(m == 0, lambda: chunk(span(fr, m), fr, m, s_relay.at[0], up))
            fu = 4 * row_up + c + (0 if first else 2)
            arrived(up_received(first, m), fu, m)
            cross(up_crosses(first, m, c), fu, m)
            if not first:
                send(m == 0, lambda: chunk(span(fu, m), fu, m, s_relay.at[1], down))

    a, odd = z // 2, z % 2
    order = [a, (a + 3 + 2 * odd) % 4, (a + 1 + 2 * odd) % 4, (a + 2) % 4]
    step_own(order[0])
    step_own(order[1])
    step_guest(order[0])
    step_own(order[2])
    step_guest(order[1])
    step_rows(order[0])
    step_own(order[3])
    step_guest(order[2])
    step_rows(order[1])
    step_guest(order[3])
    step_rows(order[2])
    step_rows(order[3])
    for second in range(2):
        fr = 4 * row_two + c + 2 * second
        arrived(True, fr, 0)
        cross(True, fr, 0)

    for j in range(PER):
        pltpu.make_async_copy(q.at[j], q.at[j], rq.at[j]).wait()
    pltpu.make_async_copy(my_rows, lists, rl.at[0]).wait()
    pltpu.make_async_copy(counts_in, counts, rl.at[1]).wait()
    for m in range(4):
        for first in (True, False):
            lane = 1 - c + (0 if first else 2)
            arrived(True, 4 * y + lane, m)
            arrived(down_crosses(first, m, 1 - c), 4 * row_down + lane, m)
            arrived(up_crosses(first, m, 1 - c), 4 * row_up + lane, m)
            if m == 0:
                arrived(True, 4 * row_two + lane, m)
    for pred, make in started:
        @pl.when(pred)
        def _():
            make().wait_send()


def attend_kernel(lists, counts, q_ref, kv_hbm, o_ref, kv, s0, s1, acc, den, sems):
    _, _, _, c, y, _, _, k = place()
    frame = 4 * y + 2 * k + c

    def loads(act):
        for fr in range(FRAMES):
            near = jnp.abs(fr - frame) <= 4

            @pl.when(near)
            def _():
                part = pl.ds(fr * PER, PER)
                act(pltpu.make_async_copy(kv_hbm.at[part], kv.at[part], sems.at[fr]))

            @pl.when(jnp.logical_not(near))
            def _():
                part = pl.ds(fr * PER, CH)
                act(pltpu.make_async_copy(kv_hbm.at[part], kv.at[part], sems.at[fr]))

    loads(lambda cp: cp.start())
    acc[...] = jnp.zeros_like(acc)
    den[...] = jnp.zeros_like(den)

    def count(i):
        return counts[0, frame * PER + i]

    total = lax.fori_loop(0, PER, lambda i, t: t + (count(i) + G - 1) // G, 0)
    loads(lambda cp: cp.wait())

    def following(i, g):
        stay = ((g + 1) * G < count(i)) | (i == PER - 1)
        return jnp.where(stay, i, i + 1), jnp.where(stay, g + 1, 0)

    def ids(i, g):
        last = count(i) - 1
        return [lists[i, jnp.minimum(g * G + u, last)] for u in range(G)]

    def score(i, g, s):
        chosen = ids(i, g)
        q = q_ref[i]
        for w in range(0, G, SUB):
            keys = jnp.concatenate([kv[t, 0] for t in chosen[w:w + SUB]], 0)
            s[:, w * TILE:(w + SUB) * TILE] = lax.dot_general(
                q, keys, (((1,), (1,)), ((), ())), preferred_element_type=f32)

    def weigh(i, g, s):
        chosen = ids(i, g)
        n = count(i)
        d = jnp.zeros((TILE, TILE), f32)
        a = jnp.zeros((TILE, HD), f32)
        for w in range(0, G, SUB):
            e = jnp.exp2(s[:, w * TILE:(w + SUB) * TILE] * SCALE)
            parts = [jnp.where(g * G + w + u < n, e[:, u * TILE:(u + 1) * TILE], 0.0) for u in range(SUB)]
            for part in parts:
                d = d + part
            weights = jnp.concatenate(parts, 1).astype(bf16)
            values = jnp.concatenate([kv[t, 1] for t in chosen[w:w + SUB]], 0)
            a = a + lax.dot_general(weights, values, (((1,), (0,)), ((), ())), preferred_element_type=f32)
        acc[i] += a
        den[i] += d

    zero = jnp.int32(0)
    score(zero, zero, s0)

    def body(_, state):
        i, g = state
        i1, g1 = following(i, g)
        score(i1, g1, s1)
        weigh(i, g, s0)
        i2, g2 = following(i1, g1)
        score(i2, g2, s0)
        weigh(i1, g1, s1)
        return i2, g2

    lax.fori_loop(0, (total + 1) // 2, body, (zero, zero))

    def finish(i, _):
        o_ref[i] = (acc[i] / jnp.sum(den[i], axis=1, keepdims=True)).astype(bf16)
        return 0

    lax.fori_loop(0, PER, finish, 0)


def return_kernel(o_in, out, send, recv):
    hd, sq, z, c, y, x, b, k = place()
    frame = 4 * y + 2 * k + c
    head = 2 * z + b
    barrier = pltpu.get_barrier_semaphore()

    def source(h):
        return 2 * (h // 2) + x % 2, 4 * y + 2 * (h % 2) + x // 2

    self_home = (frame == sq).astype(jnp.int32)
    for h in range(HEADS):
        hs, ss = source(h)

        @pl.when((hs != hd) | (ss != sq))
        def _():
            pl.semaphore_signal(barrier, 1, device_id={"head": hs, "seq": ss}, device_id_type=MESH)
    pl.semaphore_wait(barrier, HEADS - self_home)
    columns = out.at[:, pl.ds(pl.multiple_of(head * HD, HD), HD)]

    def copies(act):
        for r in range(HEADS):
            t = (hd + r) % HEADS
            remote = (t != hd) | (frame != sq)

            @pl.when(remote)
            def _():
                cp = pltpu.make_async_remote_copy(o_in.at[t], columns, send.at[r], recv.at[head],
                                                  device_id={"head": t, "seq": frame}, device_id_type=MESH)
                cp.start() if act else cp.wait_send()

            if act:
                @pl.when(jnp.logical_not(remote))
                def _():
                    pltpu.make_async_copy(o_in.at[t], columns, recv.at[head]).start()

    copies(True)
    for h in range(HEADS):
        part = out.at[:, pl.ds(h * HD, HD)]
        pltpu.make_async_copy(o_in.at[0], part, recv.at[h]).wait()
    copies(False)


def local(projected, query_gain, key_gain, tile_lists, tile_counts):
    hd = lax.axis_index("head")
    sq = lax.axis_index("seq")
    vmem = pl.BlockSpec(memory_space=pltpu.VMEM)
    smem = pl.BlockSpec(memory_space=pltpu.SMEM)
    hbm = pl.BlockSpec(memory_space=pl.ANY)
    sds = jax.ShapeDtypeStruct
    dma = pltpu.SemaphoreType.DMA
    cosine, sine = rope_tables(sq, hd)
    q_own, kv_own = pl.pallas_call(
        prepare_kernel,
        out_shape=(sds((HEADS, TILE, HD), bf16), sds((HEADS, 2, TILE, HD), bf16)),
        in_specs=[vmem] * 5,
        out_specs=(vmem, vmem),
        name="prepare",
    )(jnp.transpose(projected, (1, 0, 2)), cosine, sine, query_gain[None], key_gain[None])
    q, kv, _, lists, counts = pl.pallas_call(
        spread_kernel,
        out_shape=(sds((PER, TILE, HD), bf16), sds((FRAMES * PER, 2, TILE, HD), bf16), sds((PER, 2, TILE, HD), bf16),
                   sds((PER, 96), jnp.int32), sds((1, FRAMES * PER), jnp.int32)),
        in_specs=[hbm] * 4,
        out_specs=(hbm,) * 5,
        scratch_shapes=[dma((8,)), dma((8,)), dma((16,)), dma((16,)), dma((16,)), dma((16,)), dma((4,)), dma((4,)),
                        dma((2, 2, 4)), dma((2,)), dma((FRAMES, 4)), dma((FRAMES, 4)), dma((2,)), dma((2,))],
        compiler_params=pltpu.CompilerParams(collective_id=0, has_side_effects=True),
        name="spread",
    )(q_own, kv_own, tile_lists[0], tile_counts)
    attended = pl.pallas_call(
        attend_kernel,
        out_shape=sds((PER, TILE, HD), bf16),
        in_specs=[smem, smem, vmem, hbm],
        out_specs=vmem,
        scratch_shapes=[pltpu.VMEM((FRAMES * PER, 2, TILE, HD), bf16), pltpu.VMEM((TILE, G * TILE), f32),
                        pltpu.VMEM((TILE, G * TILE), f32), pltpu.VMEM((PER, TILE, TILE), f32),
                        pltpu.VMEM((PER, TILE, HD), f32), dma((FRAMES,))],
        compiler_params=pltpu.CompilerParams(vmem_limit_bytes=40 * 1024 * 1024),
        name="attend",
    )(lists, counts, q, kv)
    return pl.pallas_call(
        return_kernel,
        out_shape=sds((TILE, HEADS * HD), bf16),
        in_specs=[hbm],
        out_specs=hbm,
        scratch_shapes=[dma((HEADS,)), dma((HEADS,))],
        compiler_params=pltpu.CompilerParams(collective_id=1, has_side_effects=True),
        name="give_back",
    )(attended)


def solution(mesh):
    in_specs = (P(("seq", "head"), None, None), P(), P(), P("head", None, None), P("head", None))
    return jax.shard_map(local, mesh=mesh, in_specs=in_specs, out_specs=P(("seq", "head"), None), check_vma=False)
```

```python
import functools
import math

import jax
import jax.numpy as jnp
from jax import lax
from jax.experimental import pallas as pl
from jax.experimental.pallas import tpu as pltpu
from jax.sharding import PartitionSpec as P


TILE = 128
HD = 128
GW = 64
HEADS = 16
FRAMES = 16
PER = 16
CH = 4
MAXK = 96
THETA = 256.0
SCALE = math.log2(math.e) / math.sqrt(HD)
G = 16
NONE = FRAMES * PER
MESH = pl.DeviceIdType.MESH
f32 = jnp.float32
bf16 = jnp.bfloat16


def rope_tables(sq, hd):
    tokens = hd * TILE + jnp.arange(TILE, dtype=jnp.int32)
    row = tokens // GW
    column = tokens % GW
    frame = jnp.full((TILE,), sq, jnp.int32)
    first = HD // 8
    second = (HD - first) // 2
    cosines, sines = [], []
    for coordinate, extent in zip((frame, row, column), (first, second, HD - first - second)):
        middle = extent // 2
        inverse = THETA ** (-2.0 * jnp.arange(middle, dtype=f32) / extent)
        angles = coordinate.astype(f32)[:, None] * inverse[None, :]
        c, s = jnp.cos(angles), jnp.sin(angles)
        cosines += [c, c]
        sines += [-s, s]
    return jnp.concatenate(cosines, 1), jnp.concatenate(sines, 1)


def partner(field):
    lane = lax.broadcasted_iota(jnp.int32, field.shape, 1)
    first = HD // 8
    half = (HD - first) // 4
    near = jnp.where(lane < first // 2, pltpu.roll(field, HD - first // 2, 1), pltpu.roll(field, first // 2, 1))
    offset = lane - first
    lower = (offset < half) | ((offset >= 2 * half) & (offset < 3 * half))
    far = jnp.where(lower, pltpu.roll(field, HD - half, 1), pltpu.roll(field, half, 1))
    return jnp.where(lane < first, near, far)


def place():
    hd = lax.axis_index("head")
    sq = lax.axis_index("seq")
    z, c = hd // 2, hd % 2
    y, x = sq // 4, sq % 4
    b, k = x // 2, x % 2
    return hd, sq, z, c, y, x, b, k


def spread_kernel(proj, cos, sin, qg, kg, lists_in, counts_in, q, kv, transit, lists, counts,
                  kv_in, q_in, sz, st, sq_sem, rz, rt, rq, s_mate, s_far, s_y, s_relay, s_cross, arrive, sl, rl):
    hd, sq, z, c, y, x, b, k = place()
    frame = 4 * y + 2 * k + c
    started = []

    def dev(h, s):
        return {"head": h, "seq": s}

    def send(pred, make):
        @pl.when(pred)
        def _():
            make().start()
        started.append((pred, make))

    sibling = dev(2 * z + 1 - c, sq)
    mate = dev(hd, 4 * y + 2 * b + 1 - k)
    opposite = dev(hd, 4 * y + 3 - x)
    row_up, row_down, row_two = (y + 1) % 4, (y + 3) % 4, (y + 2) % 4
    up = dev(hd, 4 * row_up + x)
    down = dev(hd, 4 * row_down + x)

    barrier = pltpu.get_barrier_semaphore()
    for t in range(1, HEADS):
        pl.semaphore_signal(barrier, 1, device_id=dev((hd + t) % HEADS, sq), device_id_type=MESH)
    for device in (mate, opposite, up, down):
        pl.semaphore_signal(barrier, 1, device_id=device, device_id_type=MESH)
    for t in range(HEADS):
        @pl.when((t != hd) | (frame != sq))
        def _():
            pl.semaphore_signal(barrier, 1, device_id=dev(t, frame), device_id_type=MESH)
    self_home = (frame == sq).astype(jnp.int32)
    pl.semaphore_wait(barrier, HEADS - 1 + 4 + HEADS - self_home)

    def line(src, dst, send_sem, recv_sem, target, seq, act):
        remote = (target != hd) | (seq != sq)

        @pl.when(remote)
        def _():
            cp = pltpu.make_async_remote_copy(src, dst, send_sem, recv_sem,
                                              device_id=dev(target, seq), device_id_type=MESH)
            cp.start() if act else cp.wait_send()

        if act:
            @pl.when(jnp.logical_not(remote))
            def _():
                pltpu.make_async_copy(src, dst, recv_sem).start()

    def peer(r):
        far = (r + 1) // 2
        return (z + jnp.where(r % 2 == 1, far, 8 - far)) % 8

    def lanes(h):
        return pl.ds(pl.multiple_of(h * HD, HD), HD)

    def normed(part, gain, h):
        field = proj[part, :, lanes(h)].astype(f32)
        mean = jnp.sum(field * field, axis=1, keepdims=True) * (1.0 / HD)
        field = field * lax.rsqrt(mean + 1e-06) * gain[...]
        return (field * cos[...] + partner(field) * sin[...]).astype(bf16)

    def line_kv(r, act):
        zt = peer(r)
        for h, dst, send_sem, recv_sem in ((2 * zt + b, kv.at[sq * PER + hd], sz, rz),
                                           (2 * zt + 1 - b, transit.at[hd], st, rt)):
            if act:
                kv_in[h, 0] = normed(1, kg, h)
                kv_in[h, 1] = jnp.transpose(proj[2, :, lanes(h)])
            line(kv_in.at[h], dst, send_sem.at[r], recv_sem.at[hd], 2 * zt + k, sq, act)

    def line_q(r, act):
        zt = peer(r)
        for bb in range(2):
            h = 2 * zt + bb
            if act:
                q_in[h] = normed(0, qg, h)
            line(q_in.at[h], q.at[hd], sq_sem.at[2 * r + bb], rq.at[hd], 2 * zt + k, 4 * y + 2 * bb + b, act)

    def each(step, act):
        def body(r, _):
            step(r, act)
            return 0
        lax.fori_loop(0, 8, body, 0)

    each(line_kv, True)
    each(line_q, True)

    mine = b == c
    other_rows = lists_in.at[pl.ds((4 * y + 2 * k + 1 - c) * PER, PER)]
    my_rows = lists_in.at[pl.ds(frame * PER, PER)]
    send(mine, lambda: pltpu.make_async_remote_copy(other_rows, lists, sl.at[0], rl.at[0],
                                                    device_id=sibling, device_id_type=MESH))
    send(mine, lambda: pltpu.make_async_remote_copy(counts_in, counts, sl.at[1], rl.at[1],
                                                    device_id=sibling, device_id_type=MESH))

    @pl.when(mine)
    def _():
        pltpu.make_async_copy(my_rows, lists, rl.at[0]).start()
        pltpu.make_async_copy(counts_in, counts, rl.at[1]).start()

    def span(fr, m):
        return kv.at[pl.ds(fr * PER + m * CH, CH)]

    def chunk(src, fr, m, sem, device):
        return pltpu.make_async_remote_copy(src, span(fr, m), sem, arrive.at[fr, m],
                                            device_id=device, device_id_type=MESH)

    def arrived(pred, fr, m):
        @pl.when(pred)
        def _():
            pltpu.make_async_copy(span(fr, m), span(fr, m), arrive.at[fr, m]).wait()

    def cross(pred, fr, m):
        send(pred, lambda: chunk(span(fr, m), fr, m, s_cross.at[fr, m], sibling))

    def down_received(first, m):
        return (m == 0) | ((y > 0) & (k == 0)) if first else (m == 0) | (y > 0)

    def up_received(first, m):
        return (m == 0) | (y < 3) if first else (m == 0) | ((y < 3) & (k == 1))

    def down_crosses(first, m, core):
        if first:
            return (m == 0) | ((y > 0) & (k == 0) & (core == 1))
        return (m == 0) | ((y > 0) & ((k == 0) | (core == 1)))

    def up_crosses(first, m, core):
        if first:
            return (m == 0) | ((y < 3) & ((k == 1) | (core == 0)))
        return (m == 0) | ((y < 3) & (k == 1) & (core == 0))

    own = 4 * y + 2 * b + c
    guest = 4 * y + 2 * (1 - b) + c
    lands = k == c
    relays = k != c

    def from_here(fr, first, slot, m):
        send((m == 0) | ((y < 3) & ((k == 0) | jnp.logical_not(first))),
             lambda: chunk(span(fr, m), fr, m, s_y.at[slot, 0, m], up))
        send((m == 0) | ((y > 0) & ((k == 1) | first)),
             lambda: chunk(span(fr, m), fr, m, s_y.at[slot, 1, m], down))
        cross(True, fr, m)

    def step_own(m):
        @pl.when(lands)
        def _():
            for t in range(CH):
                j = m * CH + t
                pltpu.make_async_copy(kv.at[own * PER + j], kv.at[own * PER + j], rz.at[j]).wait()
        arrived(relays, own, m)
        send(lands, lambda: chunk(span(own, m), own, m, s_mate.at[m], mate))

        @pl.when(lands)
        def _():
            for t in range(CH):
                j = m * CH + t
                pltpu.make_async_copy(transit.at[j], transit.at[j], rt.at[j]).wait()
        send(lands, lambda: chunk(transit.at[pl.ds(m * CH, CH)], own, m, s_far.at[m], opposite))
        from_here(own, b == 0, 0, m)

    def step_guest(m):
        arrived(True, guest, m)
        send(relays, lambda: chunk(span(guest, m), guest, m, s_mate.at[m], mate))
        from_here(guest, b == 1, 1, m)

    def step_rows(m):
        for first in (True, False):
            fr = 4 * row_down + c + (0 if first else 2)
            arrived(down_received(first, m), fr, m)
            cross(down_crosses(first, m, c), fr, m)
            if first:
                send(m == 0, lambda: chunk(span(fr, m), fr, m, s_relay.at[0], up))
            fu = 4 * row_up + c + (0 if first else 2)
            arrived(up_received(first, m), fu, m)
            cross(up_crosses(first, m, c), fu, m)
            if not first:
                send(m == 0, lambda: chunk(span(fu, m), fu, m, s_relay.at[1], down))

    a, odd = z // 2, z % 2
    order = [a, (a + 3 + 2 * odd) % 4, (a + 1 + 2 * odd) % 4, (a + 2) % 4]
    step_own(order[0])
    step_own(order[1])
    step_guest(order[0])
    step_own(order[2])
    step_guest(order[1])
    step_rows(order[0])
    step_own(order[3])
    step_guest(order[2])
    step_rows(order[1])
    step_guest(order[3])
    step_rows(order[2])
    step_rows(order[3])
    for second in range(2):
        fr = 4 * row_two + c + 2 * second
        arrived(True, fr, 0)
        cross(True, fr, 0)

    for j in range(PER):
        pltpu.make_async_copy(q.at[j], q.at[j], rq.at[j]).wait()
    pltpu.make_async_copy(my_rows, lists, rl.at[0]).wait()
    pltpu.make_async_copy(counts_in, counts, rl.at[1]).wait()
    for m in range(4):
        for first in (True, False):
            lane = 1 - c + (0 if first else 2)
            arrived(True, 4 * y + lane, m)
            arrived(down_crosses(first, m, 1 - c), 4 * row_down + lane, m)
            arrived(up_crosses(first, m, 1 - c), 4 * row_up + lane, m)
            if m == 0:
                arrived(True, 4 * row_two + lane, m)
    for pred, make in started:
        @pl.when(pred)
        def _():
            make().wait_send()
    each(line_kv, False)
    each(line_q, False)


def attend_kernel(lists_hbm, counts_hbm, q_hbm, kv_hbm, o_ref, kv, q_ref, lists, counts, s0, s1, acc, ids, owner, sems):
    _, _, _, c, y, _, _, k = place()
    frame = 4 * y + 2 * k + c

    small = [pltpu.make_async_copy(src, dst, sems.at[FRAMES + n])
             for n, (src, dst) in enumerate(((lists_hbm, lists), (counts_hbm, counts), (q_hbm, q_ref)))]

    def loads(act):
        for fr in range(FRAMES):
            near = jnp.abs(fr - frame) <= 4

            @pl.when(near)
            def _():
                part = pl.ds(fr * PER, PER)
                act(pltpu.make_async_copy(kv_hbm.at[part], kv.at[part], sems.at[fr]))

            @pl.when(jnp.logical_not(near))
            def _():
                part = pl.ds(fr * PER, CH)
                act(pltpu.make_async_copy(kv_hbm.at[part], kv.at[part], sems.at[fr]))

    for cp in small:
        cp.start()
    loads(lambda cp: cp.start())
    acc[...] = jnp.zeros_like(acc)
    kv[NONE] = jnp.zeros((2, TILE, HD), bf16)
    for cp in small:
        cp.wait()

    def plan(i, e):
        n = counts[0, frame * PER + i]

        def chunk(g, e):
            owner[e] = i
            for u in range(G):
                j = g * G + u
                ids[e * G + u] = jnp.where(j < n, lists[i, j], NONE)
            return e + 1

        return lax.fori_loop(0, (n + G - 1) // G, chunk, e)

    total = lax.fori_loop(0, PER, plan, jnp.int32(0))
    owner[total] = 0
    for u in range(G):
        ids[total * G + u] = NONE
    half = (total + 1) // 2
    loads(lambda cp: cp.wait())

    def pair(e):
        return jnp.where(e < half, e, total), jnp.where(half + e < total, half + e, total)

    blank = jnp.zeros((TILE, HD), bf16)
    ones = jnp.ones((16, TILE), bf16)
    none = jnp.zeros((16, TILE), bf16)

    def score(e, s):
        left, right = pair(e)
        queries = jnp.concatenate([jnp.concatenate([q_ref[owner[left]], blank], 1),
                                   jnp.concatenate([blank, q_ref[owner[right]]], 1)], 0)
        keys = jnp.concatenate([jnp.concatenate([kv[ids[left * G + u], 0], kv[ids[right * G + u], 0]], 1)
                                for u in range(G)], 0)
        s[...] = lax.dot_general(keys, queries, (((1,), (1,)), ((), ())), preferred_element_type=f32)

    def weigh(e, s):
        for side, chunk in enumerate(pair(e)):
            weights, values, live = [], [], []
            for u in range(G):
                t = ids[chunk * G + u]
                part = s[u * TILE:(u + 1) * TILE, side * TILE:(side + 1) * TILE]
                weights.append(jnp.exp2(part * SCALE).astype(bf16))
                values.append(kv[t, 1])
                live.append(jnp.where(t < NONE, ones, none))
            rows = jnp.concatenate([jnp.concatenate(values, 1), jnp.concatenate(live, 1)], 0)
            acc[owner[chunk]] += lax.dot_general(rows, jnp.concatenate(weights, 0), (((1,), (0,)), ((), ())),
                                                 preferred_element_type=f32)

    score(jnp.int32(0), s0)

    def body(h, _):
        e = 2 * h
        score(e + 1, s1)
        weigh(e, s0)
        score(e + 2, s0)
        weigh(e + 1, s1)
        return 0

    lax.fori_loop(0, (half + 1) // 2, body, 0)

    def finish(i, _):
        o_ref[i] = jnp.transpose(acc[i, :HD] / acc[i, HD:HD + 1]).astype(bf16)
        return 0

    lax.fori_loop(0, PER, finish, 0)


def return_kernel(o_in, out, send, recv):
    hd, sq, z, c, y, x, b, k = place()
    frame = 4 * y + 2 * k + c
    head = 2 * z + b
    barrier = pltpu.get_barrier_semaphore()

    def source(h):
        return 2 * (h // 2) + x % 2, 4 * y + 2 * (h % 2) + x // 2

    self_home = (frame == sq).astype(jnp.int32)
    for h in range(HEADS):
        hs, ss = source(h)

        @pl.when((hs != hd) | (ss != sq))
        def _():
            pl.semaphore_signal(barrier, 1, device_id={"head": hs, "seq": ss}, device_id_type=MESH)
    pl.semaphore_wait(barrier, HEADS - self_home)
    columns = out.at[:, pl.ds(pl.multiple_of(head * HD, HD), HD)]

    def copies(act):
        for r in range(HEADS):
            t = (hd + r) % HEADS
            remote = (t != hd) | (frame != sq)

            @pl.when(remote)
            def _():
                cp = pltpu.make_async_remote_copy(o_in.at[t], columns, send.at[r], recv.at[head],
                                                  device_id={"head": t, "seq": frame}, device_id_type=MESH)
                cp.start() if act else cp.wait_send()

            if act:
                @pl.when(jnp.logical_not(remote))
                def _():
                    pltpu.make_async_copy(o_in.at[t], columns, recv.at[head]).start()

    copies(True)
    for h in range(HEADS):
        part = out.at[:, pl.ds(h * HD, HD)]
        pltpu.make_async_copy(o_in.at[0], part, recv.at[h]).wait()
    copies(False)


def local(projected, query_gain, key_gain, tile_lists, tile_counts):
    hd = lax.axis_index("head")
    sq = lax.axis_index("seq")
    vmem = pl.BlockSpec(memory_space=pltpu.VMEM)
    hbm = pl.BlockSpec(memory_space=pltpu.HBM)
    sds = jax.ShapeDtypeStruct
    dma = pltpu.SemaphoreType.DMA
    cosine, sine = rope_tables(sq, hd)
    q, kv, _, lists, counts = pl.pallas_call(
        spread_kernel,
        out_shape=(sds((PER, TILE, HD), bf16), sds((FRAMES * PER, 2, TILE, HD), bf16), sds((PER, 2, TILE, HD), bf16),
                   sds((PER, MAXK), jnp.int32), sds((1, FRAMES * PER), jnp.int32)),
        in_specs=[vmem] * 5 + [hbm] * 2,
        out_specs=(hbm,) * 5,
        scratch_shapes=[pltpu.VMEM((HEADS, 2, TILE, HD), bf16), pltpu.VMEM((HEADS, TILE, HD), bf16),
                        dma((8,)), dma((8,)), dma((16,)), dma((16,)), dma((16,)), dma((16,)), dma((4,)), dma((4,)),
                        dma((2, 2, 4)), dma((2,)), dma((FRAMES, 4)), dma((FRAMES, 4)), dma((2,)), dma((2,))],
        compiler_params=pltpu.CompilerParams(collective_id=0, has_side_effects=True),
        name="spread",
    )(jnp.transpose(projected, (1, 0, 2)), cosine, sine, query_gain[None], key_gain[None], tile_lists[0], tile_counts)
    chunks = PER * (MAXK // G) + 1
    attended = pl.pallas_call(
        attend_kernel,
        out_shape=sds((PER, TILE, HD), bf16),
        in_specs=[hbm] * 4,
        out_specs=vmem,
        scratch_shapes=[pltpu.VMEM((FRAMES * PER + 1, 2, TILE, HD), bf16), pltpu.VMEM((PER, TILE, HD), bf16),
                        pltpu.SMEM((PER, MAXK), jnp.int32), pltpu.SMEM((1, FRAMES * PER), jnp.int32),
                        pltpu.VMEM((G * TILE, 2 * TILE), f32), pltpu.VMEM((G * TILE, 2 * TILE), f32),
                        pltpu.VMEM((PER, HD + 16, TILE), f32), pltpu.SMEM((chunks * G,), jnp.int32),
                        pltpu.SMEM((chunks,), jnp.int32), dma((FRAMES + 3,))],
        compiler_params=pltpu.CompilerParams(vmem_limit_bytes=40 * 1024 * 1024),
        name="attend",
    )(lists, counts, q, kv)
    return pl.pallas_call(
        return_kernel,
        out_shape=sds((TILE, HEADS * HD), bf16),
        in_specs=[vmem],
        out_specs=hbm,
        scratch_shapes=[dma((HEADS,)), dma((HEADS,))],
        compiler_params=pltpu.CompilerParams(collective_id=1, has_side_effects=True),
        name="give_back",
    )(attended)


def solution(mesh):
    in_specs = (P(("seq", "head"), None, None), P(), P(), P("head", None, None), P("head", None))
    return jax.shard_map(local, mesh=mesh, in_specs=in_specs, out_specs=P(("seq", "head"), None), check_vma=False)
```

```python
import functools
import math

import jax
import jax.numpy as jnp
import numpy as np
from jax import lax
from jax.experimental import pallas as pl
from jax.experimental.pallas import tpu as pltpu
from jax.sharding import PartitionSpec as P


TILE = 128
HD = 128
GW = 64
HEADS = 16
FRAMES = 16
PER = 16
CH = 4
MAXK = 96
THETA = 256.0
SCALE = math.log2(math.e) / math.sqrt(HD)
G = 16
NONE = FRAMES * PER

MESH = pl.DeviceIdType.MESH
f32 = jnp.float32
bf16 = jnp.bfloat16


def rope_tables(sq, hd):
    first = HD // 8
    second = (HD - first) // 2
    rates = np.zeros((3, 1, HD), np.float32)
    sign = np.ones((1, HD), np.float32)
    offset = 0
    for axis, extent in enumerate((first, second, HD - first - second)):
        middle = extent // 2
        part = THETA ** (-2.0 * np.arange(middle) / extent)
        rates[axis, 0, offset:offset + extent] = np.concatenate([part, part])
        sign[0, offset:offset + middle] = -1.0
        offset += extent
    token = np.arange(TILE)[:, None]
    row = (hd * (TILE // GW) + token // GW).astype(f32)
    column = (token % GW).astype(np.float32)
    angles = sq.astype(f32) * rates[0] + row * rates[1] + column * rates[2]
    return jnp.cos(angles), jnp.sin(angles) * sign


def partner(field):
    lane = lax.broadcasted_iota(jnp.int32, field.shape, 1)
    first = HD // 8
    half = (HD - first) // 4
    near = jnp.where(lane < first // 2, pltpu.roll(field, HD - first // 2, 1), pltpu.roll(field, first // 2, 1))
    offset = lane - first
    lower = (offset < half) | ((offset >= 2 * half) & (offset < 3 * half))
    far = jnp.where(lower, pltpu.roll(field, HD - half, 1), pltpu.roll(field, half, 1))
    return jnp.where(lane < first, near, far)


def place():
    hd = lax.axis_index("head")
    sq = lax.axis_index("seq")
    z, c = hd // 2, hd % 2
    y, x = sq // 4, sq % 4
    b, k = x // 2, x % 2
    return hd, sq, z, c, y, x, b, k


def spread_kernel(proj, cos, sin, qg, kg, lists_in, counts_in, q, kv, transit, lists, counts,
                  kv_in, q_in, sz, st, sq_sem, rz, rt, rq, s_mate, s_far, s_y, s_relay, s_cross, arrive, sl, rl):
    hd, sq, z, c, y, x, b, k = place()
    frame = 4 * y + 2 * k + c
    started = []

    def dev(h, s):
        return {"head": h, "seq": s}

    def send(pred, make):
        @pl.when(pred)
        def _():
            make().start()
        started.append((pred, make))

    sibling = dev(2 * z + 1 - c, sq)
    mate = dev(hd, 4 * y + 2 * b + 1 - k)
    opposite = dev(hd, 4 * y + 3 - x)
    row_up, row_down, row_two = (y + 1) % 4, (y + 3) % 4, (y + 2) % 4
    up = dev(hd, 4 * row_up + x)
    down = dev(hd, 4 * row_down + x)

    barrier = pltpu.get_barrier_semaphore()
    for t in range(1, HEADS):
        pl.semaphore_signal(barrier, 1, device_id=dev((hd + t) % HEADS, sq), device_id_type=MESH)
    for device in (mate, opposite, up, down):
        pl.semaphore_signal(barrier, 1, device_id=device, device_id_type=MESH)
    for t in range(HEADS):
        @pl.when((t != hd) | (frame != sq))
        def _():
            pl.semaphore_signal(barrier, 1, device_id=dev(t, frame), device_id_type=MESH)
    self_home = (frame == sq).astype(jnp.int32)
    pl.semaphore_wait(barrier, HEADS - 1 + 4 + HEADS - self_home)

    def line(src, dst, send_sem, recv_sem, target, seq, act):
        remote = (target != hd) | (seq != sq)

        @pl.when(remote)
        def _():
            cp = pltpu.make_async_remote_copy(src, dst, send_sem, recv_sem,
                                              device_id=dev(target, seq), device_id_type=MESH)
            cp.start() if act else cp.wait_send()

        if act:
            @pl.when(jnp.logical_not(remote))
            def _():
                pltpu.make_async_copy(src, dst, recv_sem).start()

    def peer(r):
        far = (r + 1) // 2
        return (z + jnp.where(r % 2 == 1, far, 8 - far)) % 8

    def lanes(h):
        return pl.ds(pl.multiple_of(h * HD, HD), HD)

    def normed(part, gain, h):
        field = proj[part, :, lanes(h)].astype(f32)
        mean = jnp.sum(field * field, axis=1, keepdims=True) * (1.0 / HD)
        field = field * lax.rsqrt(mean + 1e-06) * gain[...]
        return (field * cos[...] + partner(field) * sin[...]).astype(bf16)

    def line_kv(r, act):
        zt = peer(r)
        for h, dst, send_sem, recv_sem in ((2 * zt + b, kv.at[sq * PER + hd], sz, rz),
                                           (2 * zt + 1 - b, transit.at[hd], st, rt)):
            if act:
                kv_in[h, 0] = normed(1, kg, h)
                kv_in[h, 1] = jnp.transpose(proj[2, :, lanes(h)])
            line(kv_in.at[h], dst, send_sem.at[r], recv_sem.at[hd], 2 * zt + k, sq, act)

    def line_q(r, act):
        zt = peer(r)
        for bb in range(2):
            h = 2 * zt + bb
            if act:
                q_in[h] = normed(0, qg, h)
            line(q_in.at[h], q.at[hd], sq_sem.at[2 * r + bb], rq.at[hd], 2 * zt + k, 4 * y + 2 * bb + b, act)

    def each(step, act):
        def body(r, _):
            step(r, act)
            return 0
        lax.fori_loop(0, 8, body, 0)

    each(line_kv, True)
    each(line_q, True)

    mine = b == c
    send(mine, lambda: pltpu.make_async_remote_copy(lists_in, lists, sl.at[0], rl.at[0],
                                                    device_id=sibling, device_id_type=MESH))
    send(mine, lambda: pltpu.make_async_remote_copy(counts_in, counts, sl.at[1], rl.at[1],
                                                    device_id=sibling, device_id_type=MESH))

    @pl.when(mine)
    def _():
        pltpu.make_async_copy(lists_in, lists, rl.at[0]).start()
        pltpu.make_async_copy(counts_in, counts, rl.at[1]).start()

    def span(fr, m):
        return kv.at[pl.ds(fr * PER + m * CH, CH)]

    def chunk(src, fr, m, sem, device):
        return pltpu.make_async_remote_copy(src, span(fr, m), sem, arrive.at[fr, m],
                                            device_id=device, device_id_type=MESH)

    def arrived(pred, fr, m):
        @pl.when(pred)
        def _():
            pltpu.make_async_copy(span(fr, m), span(fr, m), arrive.at[fr, m]).wait()

    def cross(pred, fr, m):
        send(pred, lambda: chunk(span(fr, m), fr, m, s_cross.at[fr, m], sibling))

    def down_received(first, m):
        return (m == 0) | ((y > 0) & (k == 0)) if first else (m == 0) | (y > 0)

    def up_received(first, m):
        return (m == 0) | (y < 3) if first else (m == 0) | ((y < 3) & (k == 1))

    def down_crosses(first, m, core):
        if first:
            return (m == 0) | ((y > 0) & (k == 0) & (core == 1))
        return (m == 0) | ((y > 0) & ((k == 0) | (core == 1)))

    def up_crosses(first, m, core):
        if first:
            return (m == 0) | ((y < 3) & ((k == 1) | (core == 0)))
        return (m == 0) | ((y < 3) & (k == 1) & (core == 0))

    own = 4 * y + 2 * b + c
    guest = 4 * y + 2 * (1 - b) + c
    lands = k == c
    relays = k != c

    def from_here(fr, first, slot, m):
        send((m == 0) | ((y < 3) & ((k == 0) | jnp.logical_not(first))),
             lambda: chunk(span(fr, m), fr, m, s_y.at[slot, 0, m], up))
        send((m == 0) | ((y > 0) & ((k == 1) | first)),
             lambda: chunk(span(fr, m), fr, m, s_y.at[slot, 1, m], down))
        cross(True, fr, m)

    def step_own(m):
        @pl.when(lands)
        def _():
            for t in range(CH):
                j = m * CH + t
                pltpu.make_async_copy(kv.at[own * PER + j], kv.at[own * PER + j], rz.at[j]).wait()
        arrived(relays, own, m)
        send(lands, lambda: chunk(span(own, m), own, m, s_mate.at[m], mate))

        @pl.when(lands)
        def _():
            for t in range(CH):
                j = m * CH + t
                pltpu.make_async_copy(transit.at[j], transit.at[j], rt.at[j]).wait()
        send(lands, lambda: chunk(transit.at[pl.ds(m * CH, CH)], own, m, s_far.at[m], opposite))
        from_here(own, b == 0, 0, m)

    def step_guest(m):
        arrived(True, guest, m)
        send(relays, lambda: chunk(span(guest, m), guest, m, s_mate.at[m], mate))
        from_here(guest, b == 1, 1, m)

    def step_rows(m):
        for first in (True, False):
            fr = 4 * row_down + c + (0 if first else 2)
            arrived(down_received(first, m), fr, m)
            cross(down_crosses(first, m, c), fr, m)
            if first:
                send(m == 0, lambda: chunk(span(fr, m), fr, m, s_relay.at[0], up))
            fu = 4 * row_up + c + (0 if first else 2)
            arrived(up_received(first, m), fu, m)
            cross(up_crosses(first, m, c), fu, m)
            if not first:
                send(m == 0, lambda: chunk(span(fu, m), fu, m, s_relay.at[1], down))

    a, odd = z // 2, z % 2
    order = [a, (a + 3 + 2 * odd) % 4, (a + 1 + 2 * odd) % 4, (a + 2) % 4]
    step_own(order[0])
    step_own(order[1])
    step_guest(order[0])
    step_own(order[2])
    step_guest(order[1])
    step_rows(order[0])
    step_own(order[3])
    step_guest(order[2])
    step_rows(order[1])
    step_guest(order[3])
    step_rows(order[2])
    step_rows(order[3])
    for second in range(2):
        fr = 4 * row_two + c + 2 * second
        arrived(True, fr, 0)
        cross(True, fr, 0)

    for j in range(PER):
        pltpu.make_async_copy(q.at[j], q.at[j], rq.at[j]).wait()
    pltpu.make_async_copy(lists_in, lists, rl.at[0]).wait()
    pltpu.make_async_copy(counts_in, counts, rl.at[1]).wait()
    for m in range(4):
        for first in (True, False):
            lane = 1 - c + (0 if first else 2)
            arrived(True, 4 * y + lane, m)
            arrived(down_crosses(first, m, 1 - c), 4 * row_down + lane, m)
            arrived(up_crosses(first, m, 1 - c), 4 * row_up + lane, m)
            if m == 0:
                arrived(True, 4 * row_two + lane, m)
    for pred, make in started:
        @pl.when(pred)
        def _():
            make().wait_send()
    each(line_kv, False)
    each(line_q, False)


def attend_kernel(lists_hbm, counts_hbm, q_hbm, kv_hbm, out, kv, q, lists, counts, s0, s1, acc, ids, done, sems,
                  send, recv):
    hd, sq, z, c, y, x, b, k = place()
    frame = 4 * y + 2 * k + c
    head = 2 * z + b

    barrier = pltpu.get_barrier_semaphore()
    self_home = (frame == sq).astype(jnp.int32)
    for h in range(HEADS):
        hs, ss = 2 * (h // 2) + k, 4 * y + 2 * (h % 2) + b

        @pl.when((hs != hd) | (ss != sq))
        def _():
            pl.semaphore_signal(barrier, 1, device_id={"head": hs, "seq": ss}, device_id_type=MESH)

    small = [pltpu.make_async_copy(src, dst, sems.at[FRAMES + n])
             for n, (src, dst) in enumerate(((lists_hbm, lists), (counts_hbm, counts), (q_hbm, q)))]

    def loads(act):
        for fr in range(FRAMES):
            near = jnp.abs(fr - frame) <= 4

            @pl.when(near)
            def _():
                part = pl.ds(fr * PER, PER)
                act(pltpu.make_async_copy(kv_hbm.at[part], kv.at[part], sems.at[fr]))

            @pl.when(jnp.logical_not(near))
            def _():
                part = pl.ds(fr * PER, CH)
                act(pltpu.make_async_copy(kv_hbm.at[part], kv.at[part], sems.at[fr]))

    for cp in small:
        cp.start()
    loads(lambda cp: cp.start())
    acc[...] = jnp.zeros_like(acc)
    kv[NONE] = jnp.zeros((2, TILE, HD), bf16)
    for cp in small:
        cp.wait()

    def plan(i, _):
        n = counts[0, frame * PER + i]
        for j in range(MAXK):
            ids[i * MAXK + j] = jnp.where(j < n, lists[j, frame * PER + i], NONE)
        return 0

    lax.fori_loop(0, PER, plan, 0)
    loads(lambda cp: cp.wait())
    pl.semaphore_wait(barrier, HEADS - self_home)

    steps = MAXK // G
    half = PER // 2
    blank = jnp.zeros((TILE, HD), bf16)
    ones = jnp.ones((16, TILE), bf16)
    none = jnp.zeros((16, TILE), bf16)

    def tiles(t):
        i = (hd + t + 1) % half
        return i, i + half

    def score(e, s):
        left, right = tiles(e // steps)
        g = (e % steps) * G
        queries = jnp.concatenate([jnp.concatenate([q[left], blank], 1), jnp.concatenate([blank, q[right]], 1)], 0)
        keys = jnp.concatenate([jnp.concatenate([kv[ids[left * MAXK + g + u], 0], kv[ids[right * MAXK + g + u], 0]], 1)
                                for u in range(G)], 0)
        s[...] = lax.dot_general(keys, queries, (((1,), (1,)), ((), ())), preferred_element_type=f32)

    def weigh(e, s):
        g = (e % steps) * G
        for side, i in enumerate(tiles(e // steps)):
            weights, values, live = [], [], []
            for u in range(G):
                t = ids[i * MAXK + g + u]
                part = s[u * TILE:(u + 1) * TILE, side * TILE:(side + 1) * TILE]
                weights.append(jnp.exp2(part * SCALE).astype(bf16))
                values.append(kv[t, 1])
                live.append(jnp.where(t < NONE, ones, none))
            rows = jnp.concatenate([jnp.concatenate(values, 1), jnp.concatenate(live, 1)], 0)
            acc[side] += lax.dot_general(rows, jnp.concatenate(weights, 0), (((1,), (0,)), ((), ())),
                                         preferred_element_type=f32)

    columns = out.at[:, pl.ds(pl.multiple_of(head * HD, HD), HD)]

    def back(t, side, act):
        i = tiles(t)[side]
        slot = 2 * t + side
        remote = (i != hd) | (frame != sq)

        @pl.when(remote)
        def _():
            cp = pltpu.make_async_remote_copy(done.at[slot], columns, send.at[slot], recv.at[head],
                                              device_id={"head": i, "seq": frame}, device_id_type=MESH)
            cp.start() if act else cp.wait_send()

        if act:
            @pl.when(jnp.logical_not(remote))
            def _():
                pltpu.make_async_copy(done.at[slot], columns, recv.at[head]).start()

    score(jnp.int32(0), s0)

    def pair(t, _):
        def body(h, _):
            e = t * steps + 2 * h
            score(e + 1, s1)
            weigh(e, s0)
            score(e + 2, s0)
            weigh(e + 1, s1)
            return 0

        lax.fori_loop(0, steps // 2, body, 0)
        for side in range(2):
            done[2 * t + side] = jnp.transpose(acc[side, :HD] / acc[side, HD:HD + 1]).astype(bf16)
            back(t, side, True)
        acc[...] = jnp.zeros_like(acc)
        return 0

    lax.fori_loop(0, half, pair, 0)
    for h in range(HEADS):
        part = out.at[:, pl.ds(h * HD, HD)]
        pltpu.make_async_copy(done.at[0], part, recv.at[h]).wait()

    def sent(t, _):
        back(t, 0, False)
        back(t, 1, False)
        return 0

    lax.fori_loop(0, half, sent, 0)


def local(projected, query_gain, key_gain, tile_lists, tile_counts):
    hd = lax.axis_index("head")
    sq = lax.axis_index("seq")
    vmem = pl.BlockSpec(memory_space=pltpu.VMEM)
    hbm = pl.BlockSpec(memory_space=pltpu.HBM)
    sds = jax.ShapeDtypeStruct
    dma = pltpu.SemaphoreType.DMA
    cosine, sine = rope_tables(sq, hd)
    q, kv, _, lists, counts = pl.pallas_call(
        spread_kernel,
        out_shape=(sds((PER, TILE, HD), bf16), sds((FRAMES * PER, 2, TILE, HD), bf16), sds((PER, 2, TILE, HD), bf16),
                   sds((MAXK, FRAMES * PER), jnp.int32), sds((1, FRAMES * PER), jnp.int32)),
        in_specs=[vmem] * 5 + [hbm] * 2,
        out_specs=(hbm,) * 5,
        scratch_shapes=[pltpu.VMEM((HEADS, 2, TILE, HD), bf16), pltpu.VMEM((HEADS, TILE, HD), bf16),
                        dma((8,)), dma((8,)), dma((16,)), dma((16,)), dma((16,)), dma((16,)), dma((4,)), dma((4,)),
                        dma((2, 2, 4)), dma((2,)), dma((FRAMES, 4)), dma((FRAMES, 4)), dma((2,)), dma((2,))],
        compiler_params=pltpu.CompilerParams(collective_id=0, has_side_effects=True),
        name="spread",
    )(jnp.transpose(projected, (1, 0, 2)), cosine, sine, query_gain[None], key_gain[None], jnp.swapaxes(tile_lists, 1, 2)[0], tile_counts)
    return pl.pallas_call(
        attend_kernel,
        out_shape=sds((TILE, HEADS * HD), bf16),
        in_specs=[hbm] * 4,
        out_specs=hbm,
        scratch_shapes=[pltpu.VMEM((FRAMES * PER + 1, 2, TILE, HD), bf16), pltpu.VMEM((PER, TILE, HD), bf16),
                        pltpu.SMEM((MAXK, FRAMES * PER), jnp.int32), pltpu.SMEM((1, FRAMES * PER), jnp.int32),
                        pltpu.VMEM((G * TILE, 2 * TILE), f32), pltpu.VMEM((G * TILE, 2 * TILE), f32),
                        pltpu.VMEM((2, HD + 16, TILE), f32), pltpu.SMEM((PER * MAXK,), jnp.int32),
                        pltpu.VMEM((PER, TILE, HD), bf16), dma((FRAMES + 3,)), dma((PER,)), dma((HEADS,))],
        compiler_params=pltpu.CompilerParams(collective_id=1, has_side_effects=True, vmem_limit_bytes=60 * 1024 * 1024),
        name="attend",
    )(lists, counts, q, kv)


def solution(mesh):
    in_specs = (P(("seq", "head"), None, None), P(), P(), P("head", None, None), P("head", None))
    return jax.shard_map(local, mesh=mesh, in_specs=in_specs, out_specs=P(("seq", "head"), None), check_vma=False)
```

```python
import functools
import math

import jax
import jax.numpy as jnp
import numpy as np
from jax import lax
from jax.experimental import pallas as pl
from jax.experimental.pallas import tpu as pltpu
from jax.sharding import PartitionSpec as P


TILE = 128
HD = 128
GW = 64
HEADS = 16
FRAMES = 16
PER = 16
CH = 4
MAXK = 96
THETA = 256.0
SCALE = math.log2(math.e) / math.sqrt(HD)
G = 16
NONE = FRAMES * PER

MESH = pl.DeviceIdType.MESH
f32 = jnp.float32
bf16 = jnp.bfloat16


def rope_rates():
    first = HD // 8
    second = (HD - first) // 2
    rates = np.zeros((8, HD), np.float32)
    rates[3] = 1.0
    offset = 0
    for axis, extent in enumerate((first, second, HD - first - second)):
        middle = extent // 2
        part = THETA ** (-2.0 * np.arange(middle) / extent)
        rates[axis, offset:offset + extent] = np.concatenate([part, part])
        rates[3, offset:offset + middle] = -1.0
        offset += extent
    return rates


def partner(field):
    lane = lax.broadcasted_iota(jnp.int32, field.shape, 1)
    first = HD // 8
    half = (HD - first) // 4
    near = jnp.where(lane < first // 2, pltpu.roll(field, HD - first // 2, 1), pltpu.roll(field, first // 2, 1))
    offset = lane - first
    lower = (offset < half) | ((offset >= 2 * half) & (offset < 3 * half))
    far = jnp.where(lower, pltpu.roll(field, HD - half, 1), pltpu.roll(field, half, 1))
    return jnp.where(lane < first, near, far)


def place():
    hd = lax.axis_index("head")
    sq = lax.axis_index("seq")
    z, c = hd // 2, hd % 2
    y, x = sq // 4, sq % 4
    b, k = x // 2, x % 2
    return hd, sq, z, c, y, x, b, k


def spread_kernel(proj, rates, qg, kg, lists_in, counts_in, q, kv, transit, lists, counts,
                  kv_in, q_in, cos, sin, sz, st, sq_sem, rz, rt, rq, s_mate, s_far, s_y, s_relay, s_cross, arrive, sl, rl):
    hd, sq, z, c, y, x, b, k = place()
    frame = 4 * y + 2 * k + c
    started = []

    def dev(h, s):
        return {"head": h, "seq": s}

    def send(pred, make):
        @pl.when(pred)
        def _():
            make().start()
        started.append((pred, make))

    sibling = dev(2 * z + 1 - c, sq)
    mate = dev(hd, 4 * y + 2 * b + 1 - k)
    opposite = dev(hd, 4 * y + 3 - x)
    row_up, row_down, row_two = (y + 1) % 4, (y + 3) % 4, (y + 2) % 4
    up = dev(hd, 4 * row_up + x)
    down = dev(hd, 4 * row_down + x)

    barrier = pltpu.get_barrier_semaphore()
    for t in range(1, HEADS):
        pl.semaphore_signal(barrier, 1, device_id=dev((hd + t) % HEADS, sq), device_id_type=MESH)
    for device in (mate, opposite, up, down):
        pl.semaphore_signal(barrier, 1, device_id=device, device_id_type=MESH)
    for t in range(HEADS):
        @pl.when((t != hd) | (frame != sq))
        def _():
            pl.semaphore_signal(barrier, 1, device_id=dev(t, frame), device_id_type=MESH)
    token = lax.broadcasted_iota(jnp.int32, (TILE, HD), 0)
    row = (hd * (TILE // GW) + token // GW).astype(f32)
    column = (token % GW).astype(f32)
    angles = sq.astype(f32) * rates[0:1] + row * rates[1:2] + column * rates[2:3]
    cos[...] = jnp.cos(angles)
    sin[...] = jnp.sin(angles) * rates[3:4]
    self_home = (frame == sq).astype(jnp.int32)
    pl.semaphore_wait(barrier, HEADS - 1 + 4 + HEADS - self_home)

    def line(src, dst, send_sem, recv_sem, target, seq, act):
        remote = (target != hd) | (seq != sq)

        @pl.when(remote)
        def _():
            cp = pltpu.make_async_remote_copy(src, dst, send_sem, recv_sem,
                                              device_id=dev(target, seq), device_id_type=MESH)
            cp.start() if act else cp.wait_send()

        if act:
            @pl.when(jnp.logical_not(remote))
            def _():
                pltpu.make_async_copy(src, dst, recv_sem).start()

    def peer(r):
        far = (r + 1) // 2
        return (z + jnp.where(r % 2 == 1, far, 8 - far)) % 8

    def lanes(h):
        return pl.ds(pl.multiple_of(h * HD, HD), HD)

    def normed(part, gain, h):
        field = proj[part, :, lanes(h)].astype(f32)
        mean = jnp.sum(field * field, axis=1, keepdims=True) * (1.0 / HD)
        field = field * lax.rsqrt(mean + 1e-06) * gain[...]
        return (field * cos[...] + partner(field) * sin[...]).astype(bf16)

    def line_kv(r, act):
        zt = peer(r)
        for h, dst, send_sem, recv_sem in ((2 * zt + b, kv.at[sq * PER + hd], sz, rz),
                                           (2 * zt + 1 - b, transit.at[hd], st, rt)):
            if act:
                kv_in[h, 0] = normed(1, kg, h)
                kv_in[h, 1] = jnp.transpose(proj[2, :, lanes(h)])
            line(kv_in.at[h], dst, send_sem.at[r], recv_sem.at[hd], 2 * zt + k, sq, act)

    def line_q(r, act):
        zt = peer(r)
        for bb in range(2):
            h = 2 * zt + bb
            if act:
                q_in[h] = normed(0, qg, h)
            line(q_in.at[h], q.at[hd], sq_sem.at[2 * r + bb], rq.at[hd], 2 * zt + k, 4 * y + 2 * bb + b, act)

    def each(step, act):
        def body(r, _):
            step(r, act)
            return 0
        lax.fori_loop(0, 8, body, 0)

    each(line_kv, True)
    each(line_q, True)

    mine = b == c
    send(mine, lambda: pltpu.make_async_remote_copy(lists_in, lists, sl.at[0], rl.at[0],
                                                    device_id=sibling, device_id_type=MESH))
    send(mine, lambda: pltpu.make_async_remote_copy(counts_in, counts, sl.at[1], rl.at[1],
                                                    device_id=sibling, device_id_type=MESH))

    @pl.when(mine)
    def _():
        pltpu.make_async_copy(lists_in, lists, rl.at[0]).start()
        pltpu.make_async_copy(counts_in, counts, rl.at[1]).start()

    def span(fr, m):
        return kv.at[pl.ds(fr * PER + m * CH, CH)]

    def chunk(src, fr, m, sem, device):
        return pltpu.make_async_remote_copy(src, span(fr, m), sem, arrive.at[fr, m],
                                            device_id=device, device_id_type=MESH)

    def arrived(pred, fr, m):
        @pl.when(pred)
        def _():
            pltpu.make_async_copy(span(fr, m), span(fr, m), arrive.at[fr, m]).wait()

    def cross(pred, fr, m):
        send(pred, lambda: chunk(span(fr, m), fr, m, s_cross.at[fr, m], sibling))

    def down_received(first, m):
        return (m == 0) | ((y > 0) & (k == 0)) if first else (m == 0) | (y > 0)

    def up_received(first, m):
        return (m == 0) | (y < 3) if first else (m == 0) | ((y < 3) & (k == 1))

    def down_crosses(first, m, core):
        if first:
            return (m == 0) | ((y > 0) & (k == 0) & (core == 1))
        return (m == 0) | ((y > 0) & ((k == 0) | (core == 1)))

    def up_crosses(first, m, core):
        if first:
            return (m == 0) | ((y < 3) & ((k == 1) | (core == 0)))
        return (m == 0) | ((y < 3) & (k == 1) & (core == 0))

    own = 4 * y + 2 * b + c
    guest = 4 * y + 2 * (1 - b) + c
    lands = k == c
    relays = k != c

    def from_here(pred, fr, first, slot, m):
        send(pred & ((m == 0) | ((y < 3) & ((k == 0) | jnp.logical_not(first)))),
             lambda: chunk(span(fr, m), fr, m, s_y.at[slot, 0, m], up))
        send(pred & ((m == 0) | ((y > 0) & ((k == 1) | first))),
             lambda: chunk(span(fr, m), fr, m, s_y.at[slot, 1, m], down))
        cross(pred, fr, m)

    def step_landing(m):
        @pl.when(lands)
        def _():
            for t in range(CH):
                j = m * CH + t
                pltpu.make_async_copy(kv.at[own * PER + j], kv.at[own * PER + j], rz.at[j]).wait()
        send(lands, lambda: chunk(span(own, m), own, m, s_mate.at[m], mate))

        @pl.when(lands)
        def _():
            for t in range(CH):
                j = m * CH + t
                pltpu.make_async_copy(transit.at[j], transit.at[j], rt.at[j]).wait()
        send(lands, lambda: chunk(transit.at[pl.ds(m * CH, CH)], own, m, s_far.at[m], opposite))
        from_here(lands, own, b == 0, 0, m)

    def step_passing(m):
        arrived(relays, guest, m)
        send(relays, lambda: chunk(span(guest, m), guest, m, s_mate.at[m], mate))
        from_here(relays, guest, b == 1, 1, m)

    def step_mate(pred, m):
        arrived(pred & lands, guest, m)
        from_here(pred & lands, guest, b == 1, 1, m)
        arrived(pred & relays, own, m)
        from_here(pred & relays, own, b == 0, 0, m)

    def step_rows(m):
        for first in (True, False):
            fr = 4 * row_down + c + (0 if first else 2)
            arrived(down_received(first, m), fr, m)
            cross(down_crosses(first, m, c), fr, m)
            if first:
                send(m == 0, lambda: chunk(span(fr, m), fr, m, s_relay.at[0], up))
            fu = 4 * row_up + c + (0 if first else 2)
            arrived(up_received(first, m), fu, m)
            cross(up_crosses(first, m, c), fu, m)
            if not first:
                send(m == 0, lambda: chunk(span(fu, m), fu, m, s_relay.at[1], down))

    a, odd = z // 2, z % 2
    order = [a, (a + 3 + 2 * odd) % 4, (a + 1 + 2 * odd) % 4, (a + 2) % 4]
    for n in range(4):
        step_landing(order[n])
        step_passing(order[n])
        step_mate(relays, order[n])
        if n >= 2:
            step_mate(lands, order[n - 2])
    step_mate(lands, order[2])
    step_mate(lands, order[3])
    for n in range(4):
        step_rows(order[n])
    for second in range(2):
        fr = 4 * row_two + c + 2 * second
        arrived(True, fr, 0)
        cross(True, fr, 0)

    for j in range(PER):
        pltpu.make_async_copy(q.at[j], q.at[j], rq.at[j]).wait()
    pltpu.make_async_copy(lists_in, lists, rl.at[0]).wait()
    pltpu.make_async_copy(counts_in, counts, rl.at[1]).wait()
    for m in range(4):
        for first in (True, False):
            lane = 1 - c + (0 if first else 2)
            arrived(True, 4 * y + lane, m)
            arrived(down_crosses(first, m, 1 - c), 4 * row_down + lane, m)
            arrived(up_crosses(first, m, 1 - c), 4 * row_up + lane, m)
            if m == 0:
                arrived(True, 4 * row_two + lane, m)
    for pred, make in started:
        @pl.when(pred)
        def _():
            make().wait_send()
    each(line_kv, False)
    each(line_q, False)


def attend_kernel(lists_hbm, counts_hbm, q_hbm, kv_hbm, out, kv, q, lists, counts, s0, s1, acc, ids, done, sems,
                  send, recv):
    hd, sq, z, c, y, x, b, k = place()
    frame = 4 * y + 2 * k + c
    head = 2 * z + b

    barrier = pltpu.get_barrier_semaphore()
    self_home = (frame == sq).astype(jnp.int32)
    for h in range(HEADS):
        hs, ss = 2 * (h // 2) + k, 4 * y + 2 * (h % 2) + b

        @pl.when((hs != hd) | (ss != sq))
        def _():
            pl.semaphore_signal(barrier, 1, device_id={"head": hs, "seq": ss}, device_id_type=MESH)

    small = [pltpu.make_async_copy(src, dst, sems.at[FRAMES + n])
             for n, (src, dst) in enumerate(((lists_hbm, lists), (counts_hbm, counts), (q_hbm, q)))]

    def loads(act):
        for fr in range(FRAMES):
            near = jnp.abs(fr - frame) <= 4

            @pl.when(near)
            def _():
                part = pl.ds(fr * PER, PER)
                act(pltpu.make_async_copy(kv_hbm.at[part], kv.at[part], sems.at[fr]))

            @pl.when(jnp.logical_not(near))
            def _():
                part = pl.ds(fr * PER, CH)
                act(pltpu.make_async_copy(kv_hbm.at[part], kv.at[part], sems.at[fr]))

    for cp in small:
        cp.start()
    loads(lambda cp: cp.start())
    acc[...] = jnp.zeros_like(acc)
    kv[NONE] = jnp.zeros((2, TILE, HD), bf16)
    for cp in small:
        cp.wait()

    def plan(i, _):
        n = counts[0, frame * PER + i]
        for j in range(MAXK):
            ids[i * MAXK + j] = jnp.where(j < n, lists[j, frame * PER + i], NONE)
        return 0

    lax.fori_loop(0, PER, plan, 0)
    loads(lambda cp: cp.wait())
    pl.semaphore_wait(barrier, HEADS - self_home)

    steps = MAXK // G
    half = PER // 2
    blank = jnp.zeros((TILE, HD), bf16)
    ones = jnp.ones((16, TILE), bf16)
    none = jnp.zeros((16, TILE), bf16)

    def tiles(t):
        i = (hd + t + 1) % half
        return i, i + half

    def score(e, s):
        left, right = tiles(e // steps)
        g = (e % steps) * G
        queries = jnp.concatenate([jnp.concatenate([q[left], blank], 1), jnp.concatenate([blank, q[right]], 1)], 0)
        keys = jnp.concatenate([jnp.concatenate([kv[ids[left * MAXK + g + u], 0], kv[ids[right * MAXK + g + u], 0]], 1)
                                for u in range(G)], 0)
        s[...] = lax.dot_general(keys, queries, (((1,), (1,)), ((), ())), preferred_element_type=f32)

    def weigh(e, s):
        g = (e % steps) * G
        for side, i in enumerate(tiles(e // steps)):
            weights, values, live = [], [], []
            for u in range(G):
                t = ids[i * MAXK + g + u]
                part = s[u * TILE:(u + 1) * TILE, side * TILE:(side + 1) * TILE]
                weights.append(jnp.exp2(part * SCALE).astype(bf16))
                values.append(kv[t, 1])
                live.append(jnp.where(t < NONE, ones, none))
            rows = jnp.concatenate([jnp.concatenate(values, 1), jnp.concatenate(live, 1)], 0)
            acc[side] += lax.dot_general(rows, jnp.concatenate(weights, 0), (((1,), (0,)), ((), ())),
                                         preferred_element_type=f32)

    columns = out.at[:, pl.ds(pl.multiple_of(head * HD, HD), HD)]

    def back(t, side, act):
        i = tiles(t)[side]
        slot = 2 * t + side
        remote = (i != hd) | (frame != sq)

        @pl.when(remote)
        def _():
            cp = pltpu.make_async_remote_copy(done.at[slot], columns, send.at[slot], recv.at[head],
                                              device_id={"head": i, "seq": frame}, device_id_type=MESH)
            cp.start() if act else cp.wait_send()

        if act:
            @pl.when(jnp.logical_not(remote))
            def _():
                pltpu.make_async_copy(done.at[slot], columns, recv.at[head]).start()

    score(jnp.int32(0), s0)

    def pair(t, _):
        def body(h, _):
            e = t * steps + 2 * h
            score(e + 1, s1)
            weigh(e, s0)
            score(e + 2, s0)
            weigh(e + 1, s1)
            return 0

        lax.fori_loop(0, steps // 2, body, 0)
        for side in range(2):
            done[2 * t + side] = jnp.transpose(acc[side, :HD] / acc[side, HD:HD + 1]).astype(bf16)
            back(t, side, True)
        acc[...] = jnp.zeros_like(acc)
        return 0

    lax.fori_loop(0, half, pair, 0)
    for h in range(HEADS):
        part = out.at[:, pl.ds(h * HD, HD)]
        pltpu.make_async_copy(done.at[0], part, recv.at[h]).wait()

    def sent(t, _):
        back(t, 0, False)
        back(t, 1, False)
        return 0

    lax.fori_loop(0, half, sent, 0)


def local(projected, query_gain, key_gain, tile_lists, tile_counts):
    vmem = pl.BlockSpec(memory_space=pltpu.VMEM)
    hbm = pl.BlockSpec(memory_space=pltpu.HBM)
    sds = jax.ShapeDtypeStruct
    dma = pltpu.SemaphoreType.DMA
    q, kv, _, lists, counts = pl.pallas_call(
        spread_kernel,
        out_shape=(sds((PER, TILE, HD), bf16), sds((FRAMES * PER, 2, TILE, HD), bf16), sds((PER, 2, TILE, HD), bf16),
                   sds((MAXK, FRAMES * PER), jnp.int32), sds((1, FRAMES * PER), jnp.int32)),
        in_specs=[vmem] * 4 + [hbm] * 2,
        out_specs=(hbm,) * 5,
        scratch_shapes=[pltpu.VMEM((HEADS, 2, TILE, HD), bf16), pltpu.VMEM((HEADS, TILE, HD), bf16),
                        pltpu.VMEM((TILE, HD), f32), pltpu.VMEM((TILE, HD), f32), dma((8,)), dma((8,)), dma((16,)), dma((16,)), dma((16,)), dma((16,)), dma((4,)), dma((4,)),
                        dma((2, 2, 4)), dma((2,)), dma((FRAMES, 4)), dma((FRAMES, 4)), dma((2,)), dma((2,))],
        compiler_params=pltpu.CompilerParams(collective_id=0, has_side_effects=True),
        name="spread",
    )(jnp.transpose(projected, (1, 0, 2)), rope_rates(), query_gain[None], key_gain[None], jnp.swapaxes(tile_lists, 1, 2)[0], tile_counts)
    return pl.pallas_call(
        attend_kernel,
        out_shape=sds((TILE, HEADS * HD), bf16),
        in_specs=[hbm] * 4,
        out_specs=hbm,
        scratch_shapes=[pltpu.VMEM((FRAMES * PER + 1, 2, TILE, HD), bf16), pltpu.VMEM((PER, TILE, HD), bf16),
                        pltpu.SMEM((MAXK, FRAMES * PER), jnp.int32), pltpu.SMEM((1, FRAMES * PER), jnp.int32),
                        pltpu.VMEM((G * TILE, 2 * TILE), f32), pltpu.VMEM((G * TILE, 2 * TILE), f32),
                        pltpu.VMEM((2, HD + 16, TILE), f32), pltpu.SMEM((PER * MAXK,), jnp.int32),
                        pltpu.VMEM((PER, TILE, HD), bf16), dma((FRAMES + 3,)), dma((PER,)), dma((HEADS,))],
        compiler_params=pltpu.CompilerParams(collective_id=1, has_side_effects=True, vmem_limit_bytes=60 * 1024 * 1024),
        name="attend",
    )(lists, counts, q, kv)


def solution(mesh):
    in_specs = (P(("seq", "head"), None, None), P(), P(), P("head", None, None), P("head", None))
    return jax.shard_map(local, mesh=mesh, in_specs=in_specs, out_specs=P(("seq", "head"), None), check_vma=False)
```

```python
import functools
import math

import jax
import jax.numpy as jnp
import numpy as np
from jax import lax
from jax.experimental import pallas as pl
from jax.experimental.pallas import tpu as pltpu
from jax.sharding import PartitionSpec as P


TILE = 128
HD = 128
GW = 64
HEADS = 16
FRAMES = 16
PER = 16
CH = 4
MAXK = 96
THETA = 256.0
SCALE = math.log2(math.e) / math.sqrt(HD)
G = 16
NONE = FRAMES * PER

MESH = pl.DeviceIdType.MESH
f32 = jnp.float32
bf16 = jnp.bfloat16


def rope_rates():
    first = HD // 8
    second = (HD - first) // 2
    rates = np.zeros((8, HD), np.float32)
    rates[3] = 1.0
    offset = 0
    for axis, extent in enumerate((first, second, HD - first - second)):
        middle = extent // 2
        part = THETA ** (-2.0 * np.arange(middle) / extent)
        rates[axis, offset:offset + extent] = np.concatenate([part, part])
        rates[3, offset:offset + middle] = -1.0
        offset += extent
    return rates


def partner(field):
    lane = lax.broadcasted_iota(jnp.int32, field.shape, 1)
    first = HD // 8
    half = (HD - first) // 4
    near = jnp.where(lane < first // 2, pltpu.roll(field, HD - first // 2, 1), pltpu.roll(field, first // 2, 1))
    offset = lane - first
    lower = (offset < half) | ((offset >= 2 * half) & (offset < 3 * half))
    far = jnp.where(lower, pltpu.roll(field, HD - half, 1), pltpu.roll(field, half, 1))
    return jnp.where(lane < first, near, far)


def place():
    hd = lax.axis_index("head")
    sq = lax.axis_index("seq")
    z, c = hd // 2, hd % 2
    y, x = sq // 4, sq % 4
    b, k = x // 2, x % 2
    return hd, sq, z, c, y, x, b, k


def attend_kernel(proj, rates, qg, kg, lists_in, counts_in, out, lists, counts,
                  kv, q, transit, kv_in, q_in, cos, sin, lists_s, counts_s, ids, s0, s1, acc, done,
                  sz, st, sq_sem, rz, rt, rq, s_mate, s_far, s_y, s_relay, s_cross, arrive, sl, rl, s_back, r_back):
    hd, sq, z, c, y, x, b, k = place()
    frame = 4 * y + 2 * k + c
    started = []

    def dev(h, s):
        return {"head": h, "seq": s}

    def send(pred, make):
        @pl.when(pred)
        def _():
            make().start()
        started.append((pred, make))

    sibling = dev(2 * z + 1 - c, sq)
    mate = dev(hd, 4 * y + 2 * b + 1 - k)
    opposite = dev(hd, 4 * y + 3 - x)
    row_up, row_down, row_two = (y + 1) % 4, (y + 3) % 4, (y + 2) % 4
    up = dev(hd, 4 * row_up + x)
    down = dev(hd, 4 * row_down + x)

    barrier = pltpu.get_barrier_semaphore()
    for t in range(1, HEADS):
        pl.semaphore_signal(barrier, 1, device_id=dev((hd + t) % HEADS, sq), device_id_type=MESH)
    for device in (mate, opposite, up, down):
        pl.semaphore_signal(barrier, 1, device_id=device, device_id_type=MESH)
    for t in range(HEADS):
        @pl.when((t != hd) | (frame != sq))
        def _():
            pl.semaphore_signal(barrier, 1, device_id=dev(t, frame), device_id_type=MESH)
    for h in range(HEADS):
        hs, ss = 2 * (h // 2) + k, 4 * y + 2 * (h % 2) + b

        @pl.when((hs != hd) | (ss != sq))
        def _():
            pl.semaphore_signal(barrier, 1, device_id=dev(hs, ss), device_id_type=MESH)
    token = lax.broadcasted_iota(jnp.int32, (TILE, HD), 0)
    row = (hd * (TILE // GW) + token // GW).astype(f32)
    column = (token % GW).astype(f32)
    angles = sq.astype(f32) * rates[0:1] + row * rates[1:2] + column * rates[2:3]
    cos[...] = jnp.cos(angles)
    sin[...] = jnp.sin(angles) * rates[3:4]
    self_home = (frame == sq).astype(jnp.int32)
    pl.semaphore_wait(barrier, HEADS - 1 + 4 + 2 * (HEADS - self_home))

    mine = b == c
    send(mine, lambda: pltpu.make_async_remote_copy(lists_in, lists, sl.at[0], rl.at[0],
                                                    device_id=sibling, device_id_type=MESH))
    send(mine, lambda: pltpu.make_async_remote_copy(counts_in, counts, sl.at[1], rl.at[1],
                                                    device_id=sibling, device_id_type=MESH))

    @pl.when(mine)
    def _():
        pltpu.make_async_copy(lists_in, lists, rl.at[0]).start()
        pltpu.make_async_copy(counts_in, counts, rl.at[1]).start()

    def line(src, dst, send_sem, recv_sem, target, seq, act):
        remote = (target != hd) | (seq != sq)

        @pl.when(remote)
        def _():
            cp = pltpu.make_async_remote_copy(src, dst, send_sem, recv_sem,
                                              device_id=dev(target, seq), device_id_type=MESH)
            cp.start() if act else cp.wait_send()

        if act:
            @pl.when(jnp.logical_not(remote))
            def _():
                pltpu.make_async_copy(src, dst, recv_sem).start()

    def peer(r):
        far = (r + 1) // 2
        return (z + jnp.where(r % 2 == 1, far, 8 - far)) % 8

    def lanes(h):
        return pl.ds(pl.multiple_of(h * HD, HD), HD)

    def normed(part, gain, h):
        field = proj[part, :, lanes(h)].astype(f32)
        mean = jnp.sum(field * field, axis=1, keepdims=True) * (1.0 / HD)
        field = field * lax.rsqrt(mean + 1e-06) * gain[...]
        return (field * cos[...] + partner(field) * sin[...]).astype(bf16)

    def line_kv(r, act):
        zt = peer(r)
        for h, dst, send_sem, recv_sem in ((2 * zt + b, kv.at[sq * PER + hd], sz, rz),
                                           (2 * zt + 1 - b, transit.at[hd], st, rt)):
            if act:
                kv_in[h, 0] = normed(1, kg, h)
                kv_in[h, 1] = jnp.transpose(proj[2, :, lanes(h)])
            line(kv_in.at[h], dst, send_sem.at[r], recv_sem.at[hd], 2 * zt + k, sq, act)

    def line_q(r, act):
        zt = peer(r)
        for bb in range(2):
            h = 2 * zt + bb
            if act:
                q_in[h] = normed(0, qg, h)
            line(q_in.at[h], q.at[hd], sq_sem.at[2 * r + bb], rq.at[hd], 2 * zt + k, 4 * y + 2 * bb + b, act)

    def each(step, act):
        def body(r, _):
            step(r, act)
            return 0
        lax.fori_loop(0, 8, body, 0)

    each(line_kv, True)
    each(line_q, True)

    pltpu.make_async_copy(lists_in, lists, rl.at[0]).wait()
    pltpu.make_async_copy(counts_in, counts, rl.at[1]).wait()
    fetch = [pltpu.make_async_copy(lists, lists_s, rl.at[2]), pltpu.make_async_copy(counts, counts_s, rl.at[3])]
    for cp in fetch:
        cp.start()
    for cp in fetch:
        cp.wait()

    def plan(i, _):
        n = counts_s[0, frame * PER + i]
        for j in range(MAXK):
            ids[i * MAXK + j] = jnp.where(j < n, lists_s[j, frame * PER + i], NONE)
        return 0

    lax.fori_loop(0, PER, plan, 0)
    acc[...] = jnp.zeros_like(acc)
    kv[NONE] = jnp.zeros((2, TILE, HD), bf16)

    def span(fr, m):
        return kv.at[pl.ds(fr * PER + m * CH, CH)]

    def chunk(src, fr, m, sem, device):
        return pltpu.make_async_remote_copy(src, span(fr, m), sem, arrive.at[fr, m],
                                            device_id=device, device_id_type=MESH)

    def arrived(pred, fr, m):
        @pl.when(pred)
        def _():
            pltpu.make_async_copy(span(fr, m), span(fr, m), arrive.at[fr, m]).wait()

    def cross(pred, fr, m):
        send(pred, lambda: chunk(span(fr, m), fr, m, s_cross.at[fr, m], sibling))

    def down_received(first, m):
        return (m == 0) | ((y > 0) & (k == 0)) if first else (m == 0) | (y > 0)

    def up_received(first, m):
        return (m == 0) | (y < 3) if first else (m == 0) | ((y < 3) & (k == 1))

    def down_crosses(first, m, core):
        if first:
            return (m == 0) | ((y > 0) & (k == 0) & (core == 1))
        return (m == 0) | ((y > 0) & ((k == 0) | (core == 1)))

    def up_crosses(first, m, core):
        if first:
            return (m == 0) | ((y < 3) & ((k == 1) | (core == 0)))
        return (m == 0) | ((y < 3) & (k == 1) & (core == 0))

    own = 4 * y + 2 * b + c
    guest = 4 * y + 2 * (1 - b) + c
    lands = k == c
    relays = k != c

    def from_here(pred, fr, first, slot, m):
        send(pred & ((m == 0) | ((y < 3) & ((k == 0) | jnp.logical_not(first)))),
             lambda: chunk(span(fr, m), fr, m, s_y.at[slot, 0, m], up))
        send(pred & ((m == 0) | ((y > 0) & ((k == 1) | first))),
             lambda: chunk(span(fr, m), fr, m, s_y.at[slot, 1, m], down))
        cross(pred, fr, m)

    def step_landing(m):
        @pl.when(lands)
        def _():
            for t in range(CH):
                j = m * CH + t
                pltpu.make_async_copy(kv.at[own * PER + j], kv.at[own * PER + j], rz.at[j]).wait()
        send(lands, lambda: chunk(span(own, m), own, m, s_mate.at[m], mate))

        @pl.when(lands)
        def _():
            for t in range(CH):
                j = m * CH + t
                pltpu.make_async_copy(transit.at[j], transit.at[j], rt.at[j]).wait()
        send(lands, lambda: chunk(transit.at[pl.ds(m * CH, CH)], own, m, s_far.at[m], opposite))
        from_here(lands, own, b == 0, 0, m)

    def step_passing(m):
        arrived(relays, guest, m)
        send(relays, lambda: chunk(span(guest, m), guest, m, s_mate.at[m], mate))
        from_here(relays, guest, b == 1, 1, m)

    def step_mate(pred, m):
        arrived(pred & lands, guest, m)
        from_here(pred & lands, guest, b == 1, 1, m)
        arrived(pred & relays, own, m)
        from_here(pred & relays, own, b == 0, 0, m)

    def step_rows(m):
        for first in (True, False):
            fr = 4 * row_down + c + (0 if first else 2)
            arrived(down_received(first, m), fr, m)
            cross(down_crosses(first, m, c), fr, m)
            if first:
                send(m == 0, lambda: chunk(span(fr, m), fr, m, s_relay.at[0], up))
            fu = 4 * row_up + c + (0 if first else 2)
            arrived(up_received(first, m), fu, m)
            cross(up_crosses(first, m, c), fu, m)
            if not first:
                send(m == 0, lambda: chunk(span(fu, m), fu, m, s_relay.at[1], down))

    a, odd = z // 2, z % 2
    order = [a, (a + 3 + 2 * odd) % 4, (a + 1 + 2 * odd) % 4, (a + 2) % 4]
    for n in range(4):
        step_landing(order[n])
        step_passing(order[n])
        step_mate(relays, order[n])
        if n >= 2:
            step_mate(lands, order[n - 2])
    step_mate(lands, order[2])
    step_mate(lands, order[3])
    for n in range(4):
        step_rows(order[n])
    for second in range(2):
        fr = 4 * row_two + c + 2 * second
        arrived(True, fr, 0)
        cross(True, fr, 0)

    for j in range(PER):
        pltpu.make_async_copy(q.at[j], q.at[j], rq.at[j]).wait()
    for m in range(4):
        for first in (True, False):
            lane = 1 - c + (0 if first else 2)
            arrived(True, 4 * y + lane, m)
            arrived(down_crosses(first, m, 1 - c), 4 * row_down + lane, m)
            arrived(up_crosses(first, m, 1 - c), 4 * row_up + lane, m)
            if m == 0:
                arrived(True, 4 * row_two + lane, m)

    steps = MAXK // G
    half = PER // 2
    blank = jnp.zeros((TILE, HD), bf16)
    ones = jnp.ones((16, TILE), bf16)
    none = jnp.zeros((16, TILE), bf16)

    def tiles(t):
        i = (hd + t + 1) % half
        return i, i + half

    def score(e, s):
        left, right = tiles(e // steps)
        g = (e % steps) * G
        queries = jnp.concatenate([jnp.concatenate([q[left], blank], 1), jnp.concatenate([blank, q[right]], 1)], 0)
        keys = jnp.concatenate([jnp.concatenate([kv[ids[left * MAXK + g + u], 0], kv[ids[right * MAXK + g + u], 0]], 1)
                                for u in range(G)], 0)
        s[...] = lax.dot_general(keys, queries, (((1,), (1,)), ((), ())), preferred_element_type=f32)

    def weigh(e, s):
        g = (e % steps) * G
        for side, i in enumerate(tiles(e // steps)):
            weights, values, live = [], [], []
            for u in range(G):
                t = ids[i * MAXK + g + u]
                part = s[u * TILE:(u + 1) * TILE, side * TILE:(side + 1) * TILE]
                weights.append(jnp.exp2(part * SCALE).astype(bf16))
                values.append(kv[t, 1])
                live.append(jnp.where(t < NONE, ones, none))
            rows = jnp.concatenate([jnp.concatenate(values, 1), jnp.concatenate(live, 1)], 0)
            acc[side] += lax.dot_general(rows, jnp.concatenate(weights, 0), (((1,), (0,)), ((), ())),
                                         preferred_element_type=f32)

    head = 2 * z + b
    columns = out.at[:, pl.ds(pl.multiple_of(head * HD, HD), HD)]

    def back(t, side, act):
        i = tiles(t)[side]
        slot = 2 * t + side
        remote = (i != hd) | (frame != sq)

        @pl.when(remote)
        def _():
            cp = pltpu.make_async_remote_copy(done.at[slot], columns, s_back.at[slot], r_back.at[head],
                                              device_id={"head": i, "seq": frame}, device_id_type=MESH)
            cp.start() if act else cp.wait_send()

        if act:
            @pl.when(jnp.logical_not(remote))
            def _():
                pltpu.make_async_copy(done.at[slot], columns, r_back.at[head]).start()

    score(jnp.int32(0), s0)

    def pair(t, _):
        def body(h, _):
            e = t * steps + 2 * h
            score(e + 1, s1)
            weigh(e, s0)
            score(e + 2, s0)
            weigh(e + 1, s1)
            return 0

        lax.fori_loop(0, steps // 2, body, 0)
        for side in range(2):
            done[2 * t + side] = jnp.transpose(acc[side, :HD] / acc[side, HD:HD + 1]).astype(bf16)
            back(t, side, True)
        acc[...] = jnp.zeros_like(acc)
        return 0

    lax.fori_loop(0, half, pair, 0)
    for h in range(HEADS):
        part = out.at[:, pl.ds(h * HD, HD)]
        pltpu.make_async_copy(done.at[0], part, r_back.at[h]).wait()

    def sent(t, _):
        back(t, 0, False)
        back(t, 1, False)
        return 0

    lax.fori_loop(0, half, sent, 0)
    for pred, make in started:
        @pl.when(pred)
        def _():
            make().wait_send()
    each(line_kv, False)
    each(line_q, False)


def local(projected, query_gain, key_gain, tile_lists, tile_counts):
    vmem = pl.BlockSpec(memory_space=pltpu.VMEM)
    hbm = pl.BlockSpec(memory_space=pltpu.HBM)
    sds = jax.ShapeDtypeStruct
    dma = pltpu.SemaphoreType.DMA
    out, _, _ = pl.pallas_call(
        attend_kernel,
        out_shape=(sds((TILE, HEADS * HD), bf16), sds((MAXK, FRAMES * PER), jnp.int32),
                   sds((1, FRAMES * PER), jnp.int32)),
        in_specs=[vmem] * 4 + [hbm] * 2,
        out_specs=(hbm,) * 3,
        scratch_shapes=[pltpu.VMEM((FRAMES * PER + 1, 2, TILE, HD), bf16), pltpu.VMEM((PER, TILE, HD), bf16),
                        pltpu.VMEM((PER, 2, TILE, HD), bf16), pltpu.VMEM((HEADS, 2, TILE, HD), bf16),
                        pltpu.VMEM((HEADS, TILE, HD), bf16), pltpu.VMEM((TILE, HD), f32), pltpu.VMEM((TILE, HD), f32),
                        pltpu.SMEM((MAXK, FRAMES * PER), jnp.int32), pltpu.SMEM((1, FRAMES * PER), jnp.int32),
                        pltpu.SMEM((PER * MAXK,), jnp.int32),
                        pltpu.VMEM((G * TILE, 2 * TILE), f32), pltpu.VMEM((G * TILE, 2 * TILE), f32),
                        pltpu.VMEM((2, HD + 16, TILE), f32), pltpu.VMEM((PER, TILE, HD), bf16),
                        dma((8,)), dma((8,)), dma((16,)), dma((16,)), dma((16,)), dma((16,)), dma((4,)), dma((4,)),
                        dma((2, 2, 4)), dma((2,)), dma((FRAMES, 4)), dma((FRAMES, 4)), dma((2,)), dma((4,)),
                        dma((PER,)), dma((HEADS,))],
        compiler_params=pltpu.CompilerParams(collective_id=0, has_side_effects=True, vmem_limit_bytes=60 * 1024 * 1024),
        name="attend",
    )(jnp.transpose(projected, (1, 0, 2)), rope_rates(), query_gain[None], key_gain[None],
      jnp.swapaxes(tile_lists, 1, 2)[0], tile_counts)
    return out


def solution(mesh):
    in_specs = (P(("seq", "head"), None, None), P(), P(), P("head", None, None), P("head", None))
    return jax.shard_map(local, mesh=mesh, in_specs=in_specs, out_specs=P(("seq", "head"), None), check_vma=False)
```

```python
import functools
import math

import jax
import jax.numpy as jnp
import numpy as np
from jax import lax
from jax.experimental import pallas as pl
from jax.experimental.pallas import tpu as pltpu
from jax.sharding import PartitionSpec as P


TILE = 128
HD = 128
GW = 64
HEADS = 16
FRAMES = 16
PER = 16
CH = 4
MAXK = 96
THETA = 256.0
SCALE = math.log2(math.e) / math.sqrt(HD)
G = 48
NONE = FRAMES * PER

MESH = pl.DeviceIdType.MESH
f32 = jnp.float32
bf16 = jnp.bfloat16


def rope_rates():
    first = HD // 8
    second = (HD - first) // 2
    rates = np.zeros((8, HD), np.float32)
    rates[3] = 1.0
    offset = 0
    for axis, extent in enumerate((first, second, HD - first - second)):
        middle = extent // 2
        part = THETA ** (-2.0 * np.arange(middle) / extent)
        rates[axis, offset:offset + extent] = np.concatenate([part, part])
        rates[3, offset:offset + middle] = -1.0
        offset += extent
    return rates


def partner(field):
    lane = lax.broadcasted_iota(jnp.int32, field.shape, 1)
    first = HD // 8
    half = (HD - first) // 4
    near = jnp.where(lane < first // 2, pltpu.roll(field, HD - first // 2, 1), pltpu.roll(field, first // 2, 1))
    offset = lane - first
    lower = (offset < half) | ((offset >= 2 * half) & (offset < 3 * half))
    far = jnp.where(lower, pltpu.roll(field, HD - half, 1), pltpu.roll(field, half, 1))
    return jnp.where(lane < first, near, far)


def place():
    hd = lax.axis_index("head")
    sq = lax.axis_index("seq")
    z, c = hd // 2, hd % 2
    y, x = sq // 4, sq % 4
    b, k = x // 2, x % 2
    return hd, sq, z, c, y, x, b, k


def attend_kernel(proj, rates, qg, kg, lists_in, counts_in, out, lists, counts,
                  kv, q, transit, kv_in, q_in, cos, sin, lists_s, counts_s, ids, s0, s1, acc, done,
                  sz, st, sq_sem, rz, rt, rq, s_mate, s_far, s_y, s_relay, s_cross, arrive, sl, rl, s_back, r_back):
    hd, sq, z, c, y, x, b, k = place()
    frame = 4 * y + 2 * k + c
    started = []

    def dev(h, s):
        return {"head": h, "seq": s}

    def send(pred, make):
        @pl.when(pred)
        def _():
            make().start()
        started.append((pred, make))

    sibling = dev(2 * z + 1 - c, sq)
    mate = dev(hd, 4 * y + 2 * b + 1 - k)
    opposite = dev(hd, 4 * y + 3 - x)
    row_up, row_down, row_two = (y + 1) % 4, (y + 3) % 4, (y + 2) % 4
    up = dev(hd, 4 * row_up + x)
    down = dev(hd, 4 * row_down + x)

    barrier = pltpu.get_barrier_semaphore()
    for t in range(1, HEADS):
        pl.semaphore_signal(barrier, 1, device_id=dev((hd + t) % HEADS, sq), device_id_type=MESH)
    for device in (mate, opposite, up, down):
        pl.semaphore_signal(barrier, 1, device_id=device, device_id_type=MESH)
    for t in range(HEADS):
        @pl.when((t != hd) | (frame != sq))
        def _():
            pl.semaphore_signal(barrier, 1, device_id=dev(t, frame), device_id_type=MESH)
    for h in range(HEADS):
        hs, ss = 2 * (h // 2) + k, 4 * y + 2 * (h % 2) + b

        @pl.when((hs != hd) | (ss != sq))
        def _():
            pl.semaphore_signal(barrier, 1, device_id=dev(hs, ss), device_id_type=MESH)
    token = lax.broadcasted_iota(jnp.int32, (TILE, HD), 0)
    row = (hd * (TILE // GW) + token // GW).astype(f32)
    column = (token % GW).astype(f32)
    angles = sq.astype(f32) * rates[0:1] + row * rates[1:2] + column * rates[2:3]
    cos[...] = jnp.cos(angles)
    sin[...] = jnp.sin(angles) * rates[3:4]
    self_home = (frame == sq).astype(jnp.int32)
    pl.semaphore_wait(barrier, HEADS - 1 + 4 + 2 * (HEADS - self_home))

    mine = b == c
    send(mine, lambda: pltpu.make_async_remote_copy(lists_in, lists, sl.at[0], rl.at[0],
                                                    device_id=sibling, device_id_type=MESH))
    send(mine, lambda: pltpu.make_async_remote_copy(counts_in, counts, sl.at[1], rl.at[1],
                                                    device_id=sibling, device_id_type=MESH))

    @pl.when(mine)
    def _():
        pltpu.make_async_copy(lists_in, lists, rl.at[0]).start()
        pltpu.make_async_copy(counts_in, counts, rl.at[1]).start()

    def line(src, dst, send_sem, recv_sem, target, seq, act):
        remote = (target != hd) | (seq != sq)

        @pl.when(remote)
        def _():
            cp = pltpu.make_async_remote_copy(src, dst, send_sem, recv_sem,
                                              device_id=dev(target, seq), device_id_type=MESH)
            cp.start() if act else cp.wait_send()

        if act:
            @pl.when(jnp.logical_not(remote))
            def _():
                pltpu.make_async_copy(src, dst, recv_sem).start()

    def peer(r):
        far = (r + 1) // 2
        return (z + jnp.where(r % 2 == 1, far, 8 - far)) % 8

    def lanes(h):
        return pl.ds(pl.multiple_of(h * HD, HD), HD)

    def normed(part, gain, h):
        field = proj[part, :, lanes(h)].astype(f32)
        mean = jnp.sum(field * field, axis=1, keepdims=True) * (1.0 / HD)
        field = field * lax.rsqrt(mean + 1e-06) * gain[...]
        return (field * cos[...] + partner(field) * sin[...]).astype(bf16)

    def line_kv(r, act):
        zt = peer(r)
        for h, dst, send_sem, recv_sem in ((2 * zt + b, kv.at[sq * PER + hd], sz, rz),
                                           (2 * zt + 1 - b, transit.at[hd], st, rt)):
            if act:
                kv_in[h, 0] = normed(1, kg, h)
                kv_in[h, 1] = jnp.transpose(proj[2, :, lanes(h)])
            line(kv_in.at[h], dst, send_sem.at[r], recv_sem.at[hd], 2 * zt + k, sq, act)

    def line_q(r, act):
        zt = peer(r)
        for bb in range(2):
            h = 2 * zt + bb
            if act:
                q_in[h] = normed(0, qg, h)
            line(q_in.at[h], q.at[hd], sq_sem.at[2 * r + bb], rq.at[hd], 2 * zt + k, 4 * y + 2 * bb + b, act)

    def each(step, act):
        def body(r, _):
            step(r, act)
            return 0
        lax.fori_loop(0, 8, body, 0)

    each(line_kv, True)

    def span(fr, m):
        return kv.at[pl.ds(fr * PER + m * CH, CH)]

    def chunk(src, fr, m, sem, device):
        return pltpu.make_async_remote_copy(src, span(fr, m), sem, arrive.at[fr, m],
                                            device_id=device, device_id_type=MESH)

    def arrived(pred, fr, m):
        @pl.when(pred)
        def _():
            pltpu.make_async_copy(span(fr, m), span(fr, m), arrive.at[fr, m]).wait()

    def cross(pred, fr, m):
        send(pred, lambda: chunk(span(fr, m), fr, m, s_cross.at[fr, m], sibling))

    def down_received(first, m):
        return (m == 0) | ((y > 0) & (k == 0)) if first else (m == 0) | (y > 0)

    def up_received(first, m):
        return (m == 0) | (y < 3) if first else (m == 0) | ((y < 3) & (k == 1))

    def down_crosses(first, m, core):
        if first:
            return (m == 0) | ((y > 0) & (k == 0) & (core == 1))
        return (m == 0) | ((y > 0) & ((k == 0) | (core == 1)))

    def up_crosses(first, m, core):
        if first:
            return (m == 0) | ((y < 3) & ((k == 1) | (core == 0)))
        return (m == 0) | ((y < 3) & (k == 1) & (core == 0))

    own = 4 * y + 2 * b + c
    guest = 4 * y + 2 * (1 - b) + c
    lands = k == c
    relays = k != c

    def from_here(pred, fr, first, slot, m):
        send(pred & ((m == 0) | ((y < 3) & ((k == 0) | jnp.logical_not(first)))),
             lambda: chunk(span(fr, m), fr, m, s_y.at[slot, 0, m], up))
        send(pred & ((m == 0) | ((y > 0) & ((k == 1) | first))),
             lambda: chunk(span(fr, m), fr, m, s_y.at[slot, 1, m], down))
        cross(pred, fr, m)

    def step_landing(m):
        @pl.when(lands)
        def _():
            for t in range(CH):
                j = m * CH + t
                pltpu.make_async_copy(kv.at[own * PER + j], kv.at[own * PER + j], rz.at[j]).wait()
        send(lands, lambda: chunk(span(own, m), own, m, s_mate.at[m], mate))

        @pl.when(lands)
        def _():
            for t in range(CH):
                j = m * CH + t
                pltpu.make_async_copy(transit.at[j], transit.at[j], rt.at[j]).wait()
        send(lands, lambda: chunk(transit.at[pl.ds(m * CH, CH)], own, m, s_far.at[m], opposite))
        from_here(lands, own, b == 0, 0, m)

    def step_passing(m):
        arrived(relays, guest, m)
        send(relays, lambda: chunk(span(guest, m), guest, m, s_mate.at[m], mate))
        from_here(relays, guest, b == 1, 1, m)

    def step_mate(pred, m):
        arrived(pred & lands, guest, m)
        from_here(pred & lands, guest, b == 1, 1, m)
        arrived(pred & relays, own, m)
        from_here(pred & relays, own, b == 0, 0, m)

    def step_rows(m):
        for first in (True, False):
            fr = 4 * row_down + c + (0 if first else 2)
            arrived(down_received(first, m), fr, m)
            cross(down_crosses(first, m, c), fr, m)
            if first:
                send(m == 0, lambda: chunk(span(fr, m), fr, m, s_relay.at[0], up))
            fu = 4 * row_up + c + (0 if first else 2)
            arrived(up_received(first, m), fu, m)
            cross(up_crosses(first, m, c), fu, m)
            if not first:
                send(m == 0, lambda: chunk(span(fu, m), fu, m, s_relay.at[1], down))

    a, odd = z // 2, z % 2
    order = [a, (a + 3 + 2 * odd) % 4, (a + 1 + 2 * odd) % 4, (a + 2) % 4]
    def make_plan():
        pltpu.make_async_copy(lists_in, lists, rl.at[0]).wait()
        pltpu.make_async_copy(counts_in, counts, rl.at[1]).wait()
        fetch = [pltpu.make_async_copy(lists, lists_s, rl.at[2]), pltpu.make_async_copy(counts, counts_s, rl.at[3])]
        for cp in fetch:
            cp.start()
        for cp in fetch:
            cp.wait()

        def plan(i, _):
            n = counts_s[0, frame * PER + i]
            for j in range(MAXK):
                ids[i * MAXK + j] = jnp.where(j < n, lists_s[j, frame * PER + i], NONE)
            return 0

        lax.fori_loop(0, PER, plan, 0)
        acc[...] = jnp.zeros_like(acc)
        kv[NONE] = jnp.zeros((2, TILE, HD), bf16)

    for n in range(4):
        step_landing(order[n])
        step_passing(order[n])
        step_mate(relays, order[n])
        if n == 0:
            each(line_q, True)
        if n == 1:
            make_plan()
        if n >= 2:
            step_mate(lands, order[n - 2])
    step_mate(lands, order[2])
    step_mate(lands, order[3])
    for n in range(4):
        step_rows(order[n])
    for second in range(2):
        fr = 4 * row_two + c + 2 * second
        arrived(True, fr, 0)
        cross(True, fr, 0)

    for j in range(PER):
        pltpu.make_async_copy(q.at[j], q.at[j], rq.at[j]).wait()
    for m in range(4):
        for first in (True, False):
            lane = 1 - c + (0 if first else 2)
            arrived(True, 4 * y + lane, m)
            arrived(down_crosses(first, m, 1 - c), 4 * row_down + lane, m)
            arrived(up_crosses(first, m, 1 - c), 4 * row_up + lane, m)
            if m == 0:
                arrived(True, 4 * row_two + lane, m)

    steps = MAXK // G
    half = PER // 2
    blank = jnp.zeros((TILE, HD), bf16)
    ones = jnp.ones((16, TILE), bf16)
    none = jnp.zeros((16, TILE), bf16)

    def tiles(t):
        i = (hd + t + 1) % half
        return i, i + half

    def score(e, s):
        left, right = tiles(e // steps)
        g = (e % steps) * G
        queries = jnp.concatenate([jnp.concatenate([q[left], blank], 1), jnp.concatenate([blank, q[right]], 1)], 0)
        keys = jnp.concatenate([jnp.concatenate([kv[ids[left * MAXK + g + u], 0], kv[ids[right * MAXK + g + u], 0]], 1)
                                for u in range(G)], 0)
        s[...] = lax.dot_general(keys, queries, (((1,), (1,)), ((), ())), preferred_element_type=f32)

    def weigh(e, s):
        g = (e % steps) * G
        for side, i in enumerate(tiles(e // steps)):
            weights, values, live = [], [], []
            for u in range(G):
                t = ids[i * MAXK + g + u]
                part = s[u * TILE:(u + 1) * TILE, side * TILE:(side + 1) * TILE]
                weights.append(jnp.exp2(part * SCALE).astype(bf16))
                values.append(kv[t, 1])
                live.append(jnp.where(t < NONE, ones, none))
            rows = jnp.concatenate([jnp.concatenate(values, 1), jnp.concatenate(live, 1)], 0)
            acc[side] += lax.dot_general(rows, jnp.concatenate(weights, 0), (((1,), (0,)), ((), ())),
                                         preferred_element_type=f32)

    head = 2 * z + b
    columns = out.at[:, pl.ds(pl.multiple_of(head * HD, HD), HD)]

    def back(t, side, act):
        i = tiles(t)[side]
        slot = 2 * t + side
        remote = (i != hd) | (frame != sq)

        @pl.when(remote)
        def _():
            cp = pltpu.make_async_remote_copy(done.at[slot], columns, s_back.at[slot], r_back.at[head],
                                              device_id={"head": i, "seq": frame}, device_id_type=MESH)
            cp.start() if act else cp.wait_send()

        if act:
            @pl.when(jnp.logical_not(remote))
            def _():
                pltpu.make_async_copy(done.at[slot], columns, r_back.at[head]).start()

    score(jnp.int32(0), s0)

    def pair(t, _):
        def body(h, _):
            e = t * steps + 2 * h
            score(e + 1, s1)
            weigh(e, s0)
            score(e + 2, s0)
            weigh(e + 1, s1)
            return 0

        lax.fori_loop(0, steps // 2, body, 0)
        for side in range(2):
            done[2 * t + side] = jnp.transpose(acc[side, :HD] / acc[side, HD:HD + 1]).astype(bf16)
            back(t, side, True)
        acc[...] = jnp.zeros_like(acc)
        return 0

    lax.fori_loop(0, half, pair, 0)
    for h in range(HEADS):
        part = out.at[:, pl.ds(h * HD, HD)]
        pltpu.make_async_copy(done.at[0], part, r_back.at[h]).wait()

    def sent(t, _):
        back(t, 0, False)
        back(t, 1, False)
        return 0

    lax.fori_loop(0, half, sent, 0)
    for pred, make in started:
        @pl.when(pred)
        def _():
            make().wait_send()
    each(line_kv, False)
    each(line_q, False)


def local(projected, query_gain, key_gain, tile_lists, tile_counts):
    vmem = pl.BlockSpec(memory_space=pltpu.VMEM)
    hbm = pl.BlockSpec(memory_space=pltpu.HBM)
    sds = jax.ShapeDtypeStruct
    dma = pltpu.SemaphoreType.DMA
    out, _, _ = pl.pallas_call(
        attend_kernel,
        out_shape=(sds((TILE, HEADS * HD), bf16), sds((MAXK, FRAMES * PER), jnp.int32),
                   sds((1, FRAMES * PER), jnp.int32)),
        in_specs=[vmem] * 4 + [hbm] * 2,
        out_specs=(hbm,) * 3,
        scratch_shapes=[pltpu.VMEM((FRAMES * PER + 1, 2, TILE, HD), bf16), pltpu.VMEM((PER, TILE, HD), bf16),
                        pltpu.VMEM((PER, 2, TILE, HD), bf16), pltpu.VMEM((HEADS, 2, TILE, HD), bf16),
                        pltpu.VMEM((HEADS, TILE, HD), bf16), pltpu.VMEM((TILE, HD), f32), pltpu.VMEM((TILE, HD), f32),
                        pltpu.SMEM((MAXK, FRAMES * PER), jnp.int32), pltpu.SMEM((1, FRAMES * PER), jnp.int32),
                        pltpu.SMEM((PER * MAXK,), jnp.int32),
                        pltpu.VMEM((G * TILE, 2 * TILE), f32), pltpu.VMEM((G * TILE, 2 * TILE), f32),
                        pltpu.VMEM((2, HD + 16, TILE), f32), pltpu.VMEM((PER, TILE, HD), bf16),
                        dma((8,)), dma((8,)), dma((16,)), dma((16,)), dma((16,)), dma((16,)), dma((4,)), dma((4,)),
                        dma((2, 2, 4)), dma((2,)), dma((FRAMES, 4)), dma((FRAMES, 4)), dma((2,)), dma((4,)),
                        dma((PER,)), dma((HEADS,))],
        compiler_params=pltpu.CompilerParams(collective_id=0, has_side_effects=True, vmem_limit_bytes=60 * 1024 * 1024),
        name="attend",
    )(jnp.transpose(projected, (1, 0, 2)), rope_rates(), query_gain[None], key_gain[None],
      jnp.swapaxes(tile_lists, 1, 2)[0], tile_counts)
    return out


def solution(mesh):
    in_specs = (P(("seq", "head"), None, None), P(), P(), P("head", None, None), P("head", None))
    return jax.shard_map(local, mesh=mesh, in_specs=in_specs, out_specs=P(("seq", "head"), None), check_vma=False)
```

```python
import functools
import math

import jax
import jax.numpy as jnp
import numpy as np
from jax import lax
from jax.experimental import pallas as pl
from jax.experimental.pallas import tpu as pltpu
from jax.sharding import PartitionSpec as P


TILE = 128
HD = 128
GW = 64
HEADS = 16
FRAMES = 16
PER = 16
CH = 4
MAXK = 96
THETA = 256.0
SCALE = math.log2(math.e) / math.sqrt(HD)
G = 48
NONE = FRAMES * PER

MESH = pl.DeviceIdType.MESH
f32 = jnp.float32
bf16 = jnp.bfloat16


def rope_rates():
    first = HD // 8
    second = (HD - first) // 2
    rates = np.zeros((8, HD), np.float32)
    rates[3] = 1.0
    offset = 0
    for axis, extent in enumerate((first, second, HD - first - second)):
        middle = extent // 2
        part = THETA ** (-2.0 * np.arange(middle) / extent)
        rates[axis, offset:offset + extent] = np.concatenate([part, part])
        rates[3, offset:offset + middle] = -1.0
        offset += extent
    return rates


def partner(field):
    lane = lax.broadcasted_iota(jnp.int32, field.shape, 1)
    first = HD // 8
    half = (HD - first) // 4
    near = jnp.where(lane < first // 2, pltpu.roll(field, HD - first // 2, 1), pltpu.roll(field, first // 2, 1))
    offset = lane - first
    lower = (offset < half) | ((offset >= 2 * half) & (offset < 3 * half))
    far = jnp.where(lower, pltpu.roll(field, HD - half, 1), pltpu.roll(field, half, 1))
    return jnp.where(lane < first, near, far)


def place():
    hd = lax.axis_index("head")
    sq = lax.axis_index("seq")
    z, c = hd // 2, hd % 2
    y, x = sq // 4, sq % 4
    b, k = x // 2, x % 2
    return hd, sq, z, c, y, x, b, k


def attend_kernel(proj, rates, qg, kg, lists_in, counts_in, out, lists, counts,
                  kv, q, transit, kv_in, q_in, cos, sin, lists_s, counts_s, ids, s0, s1, acc, done,
                  sz, st, sq_sem, rz, rt, rq, s_mate, s_far, s_y, s_relay, s_cross, arrive, sl, rl, s_back, r_back):
    hd, sq, z, c, y, x, b, k = place()
    frame = 4 * y + 2 * k + c
    started = []

    def dev(h, s):
        return {"head": h, "seq": s}

    def send(pred, make):
        @pl.when(pred)
        def _():
            make().start()
        started.append((pred, make))

    sibling = dev(2 * z + 1 - c, sq)
    mate = dev(hd, 4 * y + 2 * b + 1 - k)
    opposite = dev(hd, 4 * y + 3 - x)
    row_up, row_down, row_two = (y + 1) % 4, (y + 3) % 4, (y + 2) % 4
    up = dev(hd, 4 * row_up + x)
    down = dev(hd, 4 * row_down + x)

    barrier = pltpu.get_barrier_semaphore()
    for t in range(1, HEADS):
        pl.semaphore_signal(barrier, 1, device_id=dev((hd + t) % HEADS, sq), device_id_type=MESH)
    for device in (mate, opposite, up, down):
        pl.semaphore_signal(barrier, 1, device_id=device, device_id_type=MESH)
    for t in range(HEADS):
        @pl.when((t != hd) | (frame != sq))
        def _():
            pl.semaphore_signal(barrier, 1, device_id=dev(t, frame), device_id_type=MESH)
    for h in range(HEADS):
        hs, ss = 2 * (h // 2) + k, 4 * y + 2 * (h % 2) + b

        @pl.when((hs != hd) | (ss != sq))
        def _():
            pl.semaphore_signal(barrier, 1, device_id=dev(hs, ss), device_id_type=MESH)
    token = lax.broadcasted_iota(jnp.int32, (TILE, HD), 0)
    row = (hd * (TILE // GW) + token // GW).astype(f32)
    column = (token % GW).astype(f32)
    angles = sq.astype(f32) * rates[0:1] + row * rates[1:2] + column * rates[2:3]
    cos[...] = jnp.cos(angles)
    sin[...] = jnp.sin(angles) * rates[3:4]
    self_home = (frame == sq).astype(jnp.int32)
    pl.semaphore_wait(barrier, HEADS - 1 + 4 + 2 * (HEADS - self_home))

    mine = b == c
    send(mine, lambda: pltpu.make_async_remote_copy(lists_in, lists, sl.at[0], rl.at[0],
                                                    device_id=sibling, device_id_type=MESH))
    send(mine, lambda: pltpu.make_async_remote_copy(counts_in, counts, sl.at[1], rl.at[1],
                                                    device_id=sibling, device_id_type=MESH))

    @pl.when(mine)
    def _():
        pltpu.make_async_copy(lists_in, lists, rl.at[0]).start()
        pltpu.make_async_copy(counts_in, counts, rl.at[1]).start()

    def line(src, dst, send_sem, recv_sem, target, seq, act):
        remote = (target != hd) | (seq != sq)

        @pl.when(remote)
        def _():
            cp = pltpu.make_async_remote_copy(src, dst, send_sem, recv_sem,
                                              device_id=dev(target, seq), device_id_type=MESH)
            cp.start() if act else cp.wait_send()

        if act:
            @pl.when(jnp.logical_not(remote))
            def _():
                pltpu.make_async_copy(src, dst, recv_sem).start()

    def peer(r):
        far = (r + 1) // 2
        return (z + jnp.where(r % 2 == 1, far, 8 - far)) % 8

    def lanes(h):
        return pl.ds(pl.multiple_of(h * HD, HD), HD)

    def normed(part, gain, h):
        field = proj[part, :, lanes(h)].astype(f32)
        mean = jnp.sum(field * field, axis=1, keepdims=True) * (1.0 / HD)
        field = field * lax.rsqrt(mean + 1e-06) * gain[...]
        return (field * cos[...] + partner(field) * sin[...]).astype(bf16)

    def line_kv(r, act):
        zt = peer(r)
        for h, dst, send_sem, recv_sem in ((2 * zt + b, kv.at[sq * PER + hd], sz, rz),
                                           (2 * zt + 1 - b, transit.at[hd], st, rt)):
            if act:
                kv_in[h, 0] = normed(1, kg, h)
                kv_in[h, 1] = jnp.transpose(proj[2, :, lanes(h)])
            line(kv_in.at[h], dst, send_sem.at[r], recv_sem.at[hd], 2 * zt + k, sq, act)

    def line_q(r, act):
        zt = peer(r)
        for bb in range(2):
            h = 2 * zt + bb
            if act:
                q_in[h] = normed(0, qg, h)
            line(q_in.at[h], q.at[hd], sq_sem.at[2 * r + bb], rq.at[hd], 2 * zt + k, 4 * y + 2 * bb + b, act)

    def each(step, act):
        def body(r, _):
            step(r, act)
            return 0
        lax.fori_loop(0, 8, body, 0)

    each(line_kv, True)

    def span(fr, m):
        return kv.at[pl.ds(fr * PER + m * CH, CH)]

    def chunk(src, fr, m, sem, device):
        return pltpu.make_async_remote_copy(src, span(fr, m), sem, arrive.at[fr, m],
                                            device_id=device, device_id_type=MESH)

    def arrived(pred, fr, m):
        @pl.when(pred)
        def _():
            pltpu.make_async_copy(span(fr, m), span(fr, m), arrive.at[fr, m]).wait()

    def cross(pred, fr, m):
        send(pred, lambda: chunk(span(fr, m), fr, m, s_cross.at[fr, m], sibling))

    def down_received(first, m):
        return (m == 0) | ((y > 0) & (k == 0)) if first else (m == 0) | (y > 0)

    def up_received(first, m):
        return (m == 0) | (y < 3) if first else (m == 0) | ((y < 3) & (k == 1))

    def down_crosses(first, m, core):
        if first:
            return (m == 0) | ((y > 0) & (k == 0) & (core == 1))
        return (m == 0) | ((y > 0) & ((k == 0) | (core == 1)))

    def up_crosses(first, m, core):
        if first:
            return (m == 0) | ((y < 3) & ((k == 1) | (core == 0)))
        return (m == 0) | ((y < 3) & (k == 1) & (core == 0))

    own = 4 * y + 2 * b + c
    guest = 4 * y + 2 * (1 - b) + c
    lands = k == c
    relays = k != c

    def from_here(pred, fr, first, slot, m):
        send(pred & ((m == 0) | ((y < 3) & ((k == 0) | jnp.logical_not(first)))),
             lambda: chunk(span(fr, m), fr, m, s_y.at[slot, 0, m], up))
        send(pred & ((m == 0) | ((y > 0) & ((k == 1) | first))),
             lambda: chunk(span(fr, m), fr, m, s_y.at[slot, 1, m], down))
        cross(pred, fr, m)

    def step_landing(m):
        @pl.when(lands)
        def _():
            for t in range(CH):
                j = m * CH + t
                pltpu.make_async_copy(kv.at[own * PER + j], kv.at[own * PER + j], rz.at[j]).wait()
        send(lands, lambda: chunk(span(own, m), own, m, s_mate.at[m], mate))

        @pl.when(lands)
        def _():
            for t in range(CH):
                j = m * CH + t
                pltpu.make_async_copy(transit.at[j], transit.at[j], rt.at[j]).wait()
        send(lands, lambda: chunk(transit.at[pl.ds(m * CH, CH)], own, m, s_far.at[m], opposite))
        from_here(lands, own, b == 0, 0, m)

    def step_passing(m):
        arrived(relays, guest, m)
        send(relays, lambda: chunk(span(guest, m), guest, m, s_mate.at[m], mate))
        from_here(relays, guest, b == 1, 1, m)

    def step_mate(pred, m):
        arrived(pred & lands, guest, m)
        from_here(pred & lands, guest, b == 1, 1, m)
        arrived(pred & relays, own, m)
        from_here(pred & relays, own, b == 0, 0, m)

    def step_rows(m):
        for first in (True, False):
            fr = 4 * row_down + c + (0 if first else 2)
            arrived(down_received(first, m), fr, m)
            cross(down_crosses(first, m, c), fr, m)
            if first:
                send(m == 0, lambda: chunk(span(fr, m), fr, m, s_relay.at[0], up))
            fu = 4 * row_up + c + (0 if first else 2)
            arrived(up_received(first, m), fu, m)
            cross(up_crosses(first, m, c), fu, m)
            if not first:
                send(m == 0, lambda: chunk(span(fu, m), fu, m, s_relay.at[1], down))

    a, odd = z // 2, z % 2
    order = [a, (a + 3 + 2 * odd) % 4, (a + 1 + 2 * odd) % 4, (a + 2) % 4]
    def make_plan():
        pltpu.make_async_copy(lists_in, lists, rl.at[0]).wait()
        pltpu.make_async_copy(counts_in, counts, rl.at[1]).wait()
        fetch = [pltpu.make_async_copy(lists, lists_s, rl.at[2]), pltpu.make_async_copy(counts, counts_s, rl.at[3])]
        for cp in fetch:
            cp.start()
        for cp in fetch:
            cp.wait()

        def plan(i, _):
            n = counts_s[0, frame * PER + i]
            for j in range(MAXK):
                ids[i * MAXK + j] = jnp.where(j < n, lists_s[j, frame * PER + i], NONE)
            return 0

        lax.fori_loop(0, PER, plan, 0)
        acc[...] = jnp.zeros_like(acc)
        kv[NONE] = jnp.zeros((2, TILE, HD), bf16)

    for n in range(4):
        step_landing(order[n])
        step_passing(order[n])
        step_mate(relays, order[n])
        if n == 0:
            each(line_q, True)
        if n == 1:
            make_plan()
        if n >= 2:
            step_mate(lands, order[n - 2])
    step_rows(order[0])
    step_mate(lands, order[2])
    step_rows(order[1])
    step_mate(lands, order[3])
    step_rows(order[2])
    step_rows(order[3])
    for second in range(2):
        fr = 4 * row_two + c + 2 * second
        arrived(True, fr, 0)
        cross(True, fr, 0)

    for j in range(PER):
        pltpu.make_async_copy(q.at[j], q.at[j], rq.at[j]).wait()
    for m in range(4):
        for first in (True, False):
            lane = 1 - c + (0 if first else 2)
            arrived(True, 4 * y + lane, m)
            arrived(down_crosses(first, m, 1 - c), 4 * row_down + lane, m)
            arrived(up_crosses(first, m, 1 - c), 4 * row_up + lane, m)
            if m == 0:
                arrived(True, 4 * row_two + lane, m)

    steps = MAXK // G
    half = PER // 2
    blank = jnp.zeros((TILE, HD), bf16)
    ones = jnp.ones((16, TILE), bf16)
    none = jnp.zeros((16, TILE), bf16)

    def tiles(t):
        i = (hd + t + 1) % half
        return i, i + half

    def score(e, s):
        left, right = tiles(e // steps)
        g = (e % steps) * G
        queries = jnp.concatenate([jnp.concatenate([q[left], blank], 1), jnp.concatenate([blank, q[right]], 1)], 0)
        keys = jnp.concatenate([jnp.concatenate([kv[ids[left * MAXK + g + u], 0], kv[ids[right * MAXK + g + u], 0]], 1)
                                for u in range(G)], 0)
        s[...] = lax.dot_general(keys, queries, (((1,), (1,)), ((), ())), preferred_element_type=f32)

    def weigh(e, s):
        g = (e % steps) * G
        for side, i in enumerate(tiles(e // steps)):
            weights, values, live = [], [], []
            for u in range(G):
                t = ids[i * MAXK + g + u]
                part = s[u * TILE:(u + 1) * TILE, side * TILE:(side + 1) * TILE]
                weights.append(jnp.exp2(part * SCALE).astype(bf16))
                values.append(kv[t, 1])
                live.append(jnp.where(t < NONE, ones, none))
            rows = jnp.concatenate([jnp.concatenate(values, 1), jnp.concatenate(live, 1)], 0)
            acc[side] += lax.dot_general(rows, jnp.concatenate(weights, 0), (((1,), (0,)), ((), ())),
                                         preferred_element_type=f32)

    head = 2 * z + b
    columns = out.at[:, pl.ds(pl.multiple_of(head * HD, HD), HD)]

    def back(t, side, act):
        i = tiles(t)[side]
        slot = 2 * t + side
        remote = (i != hd) | (frame != sq)

        @pl.when(remote)
        def _():
            cp = pltpu.make_async_remote_copy(done.at[slot], columns, s_back.at[slot], r_back.at[head],
                                              device_id={"head": i, "seq": frame}, device_id_type=MESH)
            cp.start() if act else cp.wait_send()

        if act:
            @pl.when(jnp.logical_not(remote))
            def _():
                pltpu.make_async_copy(done.at[slot], columns, r_back.at[head]).start()

    score(jnp.int32(0), s0)

    def pair(t, _):
        def body(h, _):
            e = t * steps + 2 * h
            score(e + 1, s1)
            weigh(e, s0)
            score(e + 2, s0)
            weigh(e + 1, s1)
            return 0

        lax.fori_loop(0, steps // 2, body, 0)
        for side in range(2):
            done[2 * t + side] = jnp.transpose(acc[side, :HD] / acc[side, HD:HD + 1]).astype(bf16)
            back(t, side, True)
        acc[...] = jnp.zeros_like(acc)
        return 0

    lax.fori_loop(0, half, pair, 0)
    for h in range(HEADS):
        part = out.at[:, pl.ds(h * HD, HD)]
        pltpu.make_async_copy(done.at[0], part, r_back.at[h]).wait()

    def sent(t, _):
        back(t, 0, False)
        back(t, 1, False)
        return 0

    lax.fori_loop(0, half, sent, 0)
    for pred, make in started:
        @pl.when(pred)
        def _():
            make().wait_send()
    each(line_kv, False)
    each(line_q, False)


def local(projected, query_gain, key_gain, tile_lists, tile_counts):
    vmem = pl.BlockSpec(memory_space=pltpu.VMEM)
    hbm = pl.BlockSpec(memory_space=pltpu.HBM)
    sds = jax.ShapeDtypeStruct
    dma = pltpu.SemaphoreType.DMA
    out, _, _ = pl.pallas_call(
        attend_kernel,
        out_shape=(sds((TILE, HEADS * HD), bf16), sds((MAXK, FRAMES * PER), jnp.int32),
                   sds((1, FRAMES * PER), jnp.int32)),
        in_specs=[vmem] * 4 + [hbm] * 2,
        out_specs=(hbm,) * 3,
        scratch_shapes=[pltpu.VMEM((FRAMES * PER + 1, 2, TILE, HD), bf16), pltpu.VMEM((PER, TILE, HD), bf16),
                        pltpu.VMEM((PER, 2, TILE, HD), bf16), pltpu.VMEM((HEADS, 2, TILE, HD), bf16),
                        pltpu.VMEM((HEADS, TILE, HD), bf16), pltpu.VMEM((TILE, HD), f32), pltpu.VMEM((TILE, HD), f32),
                        pltpu.SMEM((MAXK, FRAMES * PER), jnp.int32), pltpu.SMEM((1, FRAMES * PER), jnp.int32),
                        pltpu.SMEM((PER * MAXK,), jnp.int32),
                        pltpu.VMEM((G * TILE, 2 * TILE), f32), pltpu.VMEM((G * TILE, 2 * TILE), f32),
                        pltpu.VMEM((2, HD + 16, TILE), f32), pltpu.VMEM((PER, TILE, HD), bf16),
                        dma((8,)), dma((8,)), dma((16,)), dma((16,)), dma((16,)), dma((16,)), dma((4,)), dma((4,)),
                        dma((2, 2, 4)), dma((2,)), dma((FRAMES, 4)), dma((FRAMES, 4)), dma((2,)), dma((4,)),
                        dma((PER,)), dma((HEADS,))],
        compiler_params=pltpu.CompilerParams(collective_id=0, has_side_effects=True, vmem_limit_bytes=60 * 1024 * 1024),
        name="attend",
    )(jnp.transpose(projected, (1, 0, 2)), rope_rates(), query_gain[None], key_gain[None],
      jnp.swapaxes(tile_lists, 1, 2)[0], tile_counts)
    return out


def solution(mesh):
    in_specs = (P(("seq", "head"), None, None), P(), P(), P("head", None, None), P("head", None))
    return jax.shard_map(local, mesh=mesh, in_specs=in_specs, out_specs=P(("seq", "head"), None), check_vma=False)
```
